32 devices in a mesh: grp: 2 (over x), ctx: 16 (over z, y, core).
Axes of the slice: x: 2, y: 2, z: 4, core: 2. Of those that a mesh axis runs over, the one named last changes fastest.
Arguments:
- queries: bfloat16 [8192, 1024], P(('grp', 'ctx')), parts along dimension 0, may hold values from -10 to 10
- keys: bfloat16 [8192, 1024], P(('grp', 'ctx')), parts along dimension 0, may hold values from -10 to 10
- values: bfloat16 [8192, 1024], P(('grp', 'ctx')), parts along dimension 0, may hold values from -6 to 6
- out_grad: bfloat16 [8192, 1024], P(('grp', 'ctx')), parts along dimension 0, may hold values from -6 to 6
- key_blocks: int32 [64, 8], P(('grp', 'ctx')), parts along dimension 0, may hold values from -1 to 30, as said below
- path_length: int32 [2], P('grp'), parts along dimension 0, may hold values from 3968 to 4096
Outputs:
- attended: bfloat16 [8192, 1024], P(('grp', 'ctx')), parts along dimension 0
- grad_q: bfloat16 [8192, 1024], P(('grp', 'ctx')), parts along dimension 0
- grad_k: bfloat16 [8192, 1024], P(('grp', 'ctx')), parts along dimension 0
- grad_v: bfloat16 [8192, 1024], P(('grp', 'ctx')), parts along dimension 0
The draws below stay inside these ranges and needn't reach their ends.
There are 2 independent parts, one for each index of `grp`. The reference program is written for one: setup_inputs(seed, part) draws one part's arguments, and reference() takes and returns one part's arrays. A program takes and returns all parts, laid end to end along the dimension named above; each array names one. Nothing has to cross between parts.
Inputs may be any that keep to these rules, and one draw needn't show every extreme that they name: `key_blocks`: entry j of row b is b - 2**j or -1; it is -1 where b - 2**j < 0. Blocks held by the last device of ctx keep every entry that is not negative.
All inputs are finite; a program needn't handle non-finite values.
Results may differ from the reference program's by a relative error of at most 0.0028.
The reference program's roundings to bfloat16 on the way (of `weights_low` and `score_grad`) count: a program that leaves them out, or rounds other values in their place, can miss the bound.
Values may be sent and summed in bfloat16 or wider, within the bound.
No kernel may reach another device: no remote copies, remote signals or barrier semaphores. Data moves between devices by JAX's collectives and lax.ppermute only.
A program may use at most 128 MiB of HBM per device.

```python
import jax
import jax.numpy as jnp
from jax import lax

HEADS = 8
HEAD_DIM = 128
BLOCK = 128
LEVELS = 8
TOK_DEV = 256
SEQ = 4096
BLOCKS = 32


def draw_queries(key, part):
    shape = (SEQ, HEADS * HEAD_DIM)
    base = jnp.clip(2.0 * jax.random.normal(jax.random.fold_in(key, 11), shape, jnp.float32), -9.0, 9.0)
    return base.astype(jnp.bfloat16)


def draw_keys(key, part):
    shape = (SEQ, HEADS * HEAD_DIM)
    base = jnp.clip(jax.random.normal(jax.random.fold_in(key, 13), shape, jnp.float32), -6.0, 6.0)
    return base.astype(jnp.bfloat16)


def draw_key_blocks(key, part):
    key = jax.random.fold_in(key, 21)
    rows = jnp.arange(BLOCKS, dtype=jnp.int32)[:, None]
    level_index = jnp.arange(LEVELS, dtype=jnp.int32)[None, :]
    target = rows - jnp.int32(2) ** level_index
    coin = jax.random.randint(key, (BLOCKS, LEVELS), 0, 2).astype(jnp.int32)
    last_rows = rows >= BLOCKS - TOK_DEV // BLOCK
    keep = (target >= 0) & ((coin == 1) | last_rows)
    return jnp.where(keep, target, -1).astype(jnp.int32)


def shard_levels(stream_key, shape, shards, low, high):
    def one(axis_at, blocks):
        heights = jax.random.uniform(jax.random.fold_in(jax.random.fold_in(stream_key, 6), axis_at), (blocks,), jnp.float32, low / len(shards), high / len(shards))
        return jnp.repeat(jnp.exp(heights), shape[axis_at] // blocks).reshape((-1,) + (1,) * (len(shape) - axis_at - 1))

    gain = one(*shards[0])
    for cut in shards[1:]:
        gain = gain * one(*cut)
    return gain


def noise(rng, extent, width, most, pieces=(), kind=jnp.bfloat16):
    entries = width * jax.random.normal(rng, extent, jnp.float32)
    if pieces:
        entries = entries * shard_levels(rng, extent, pieces, -0.22, 0.18)
    return jnp.clip(entries, -most, most).astype(kind)


def setup_inputs(seed: int = 0, part: int = 0) -> dict:
    arg_keys = jax.random.split(jax.random.key(seed), 7)
    part_splits = jax.random.split(jax.random.fold_in(arg_keys[6], part), 7)
    queries = draw_queries(jax.random.fold_in(jax.random.fold_in(arg_keys[6], part), 71), part)
    keys = draw_keys(jax.random.fold_in(jax.random.fold_in(arg_keys[6], part), 71), part)
    values = noise(part_splits[2], (SEQ, HEADS * HEAD_DIM), 1.0, 6.0, ((0, 16),))
    out_grad = noise(part_splits[3], (SEQ, HEADS * HEAD_DIM), 1.0, 6.0, ((0, 16),))
    key_blocks = draw_key_blocks(jax.random.fold_in(jax.random.fold_in(arg_keys[6], part), 71), part)
    path_length = jax.random.randint(part_splits[5], (1,), SEQ - TOK_DEV // 2, SEQ + 1).astype(jnp.int32)
    return {"queries": queries, "keys": keys, "values": values, "out_grad": out_grad, "key_blocks": key_blocks, "path_length": path_length}


def reference(queries, keys, values, out_grad, key_blocks, path_length):
    valid_steps = path_length[0]
    score_scale = HEAD_DIM ** -0.5

    def split_blocks(array):
        return array.reshape(BLOCKS, BLOCK, HEADS, HEAD_DIM)

    query_blocks = split_blocks(queries)
    key_cells = split_blocks(keys)
    value_cells = split_blocks(values)
    grad_blocks = split_blocks(out_grad)
    places = jnp.arange(SEQ, dtype=jnp.int32).reshape(BLOCKS, BLOCK)
    level_order = jnp.arange(LEVELS + 1, dtype=jnp.int32)

    def visit(carried, block_index):
        key_total, value_total = carried
        chosen = jnp.concatenate([block_index[None], key_blocks[block_index]]).astype(jnp.int32)
        usable = chosen >= 0
        safe_index = jnp.maximum(chosen, 0).astype(jnp.int32)
        key_taken = key_cells[safe_index].astype(jnp.float32)
        value_taken = value_cells[safe_index].astype(jnp.float32)
        query_here = query_blocks[block_index].astype(jnp.float32)
        grad_here = grad_blocks[block_index].astype(jnp.float32)
        query_step = places[block_index]
        key_step = places[safe_index]
        causal = (level_order[None, :, None] > 0) | (key_step[None, :, :] <= query_step[:, None, None])
        allowed = usable[None, :, None] & (key_step[None, :, :] < valid_steps) & causal
        allowed = allowed & (query_step < valid_steps)[:, None, None]
        scores = jnp.einsum("ihd,jthd->hijt", query_here, key_taken) * score_scale
        row_max = jnp.max(jnp.where(allowed[None], scores, -1e30), axis=(2, 3), keepdims=True)
        raw_weights = jnp.where(allowed[None], jnp.exp(scores - row_max), 0.0)
        row_total = jnp.sum(raw_weights, axis=(2, 3), keepdims=True)
        row_ok = (query_step < valid_steps)[None, :, None, None]
        weights = raw_weights / jnp.where(row_ok, row_total, 1.0)
        weights_low = weights.astype(jnp.bfloat16).astype(jnp.float32)
        attended = jnp.einsum("hijt,jthd->ihd", weights_low, value_taken).astype(jnp.bfloat16)
        row_delta = jnp.sum(grad_here * attended.astype(jnp.float32), axis=2)
        row_delta = row_delta.T[:, :, None, None]
        weight_grad = jnp.einsum("ihd,jthd->hijt", grad_here, value_taken)
        score_grad = (weights * (weight_grad - row_delta)).astype(jnp.bfloat16).astype(jnp.float32)
        query_grad = (jnp.einsum("hijt,jthd->ihd", score_grad, key_taken) * score_scale).astype(jnp.bfloat16)
        key_part = jnp.einsum("hijt,ihd->jthd", score_grad, query_here) * score_scale
        value_part = jnp.einsum("hijt,ihd->jthd", weights_low, grad_here)
        key_total = key_total.at[safe_index].add(key_part)
        value_total = value_total.at[safe_index].add(value_part)
        return (key_total, value_total), (attended, query_grad)

    empty = jnp.zeros((BLOCKS, BLOCK, HEADS, HEAD_DIM), jnp.float32)
    (key_total, value_total), (attended, query_grad) = lax.scan(
        visit, (empty, empty), jnp.arange(BLOCKS, dtype=jnp.int32))
    flat = (SEQ, HEADS * HEAD_DIM)
    return (attended.reshape(flat), query_grad.reshape(flat),
            key_total.reshape(flat).astype(jnp.bfloat16), value_total.reshape(flat).astype(jnp.bfloat16))
```

```python
import functools
import math

import jax
import jax.numpy as jnp
from jax import lax
from jax.experimental import pallas as pl
from jax.experimental.pallas import tpu as pltpu
from jax.sharding import PartitionSpec as P

HEAD_DIM = 128
BLOCK = 128
LEVELS = 8
CHUNKS = 2
HEADS_STEP = 2
FAR = 1e30
SCALE = HEAD_DIM ** (-0.5)
SCALE2 = SCALE * math.log2(math.e)


def product_rows(left, right):
    return lax.dot_general(
        left, right, (((1,), (1,)), ((), ())), preferred_element_type=jnp.float32
    )


def product(left, right):
    return jnp.dot(left, right, preferred_element_type=jnp.float32)


def head_columns(array, head):
    return array[:, head * HEAD_DIM : (head + 1) * HEAD_DIM]


def block_rows(array, index):
    return array[index * BLOCK : (index + 1) * BLOCK]


def query_kernel(hops, fresh, info, kb, q_ref, k_ref, v_ref, g_ref, *refs):
    behind = refs[: len(hops)]
    att_ref, dq_ref, stat_ref, bias_ref = refs[-4:]
    step = pl.program_id(0)
    device, valid = info[0], info[1]
    pieces = 2 + len(hops)

    def rows_ok(block):
        at = (device * 2 + block) * BLOCK
        return at + lax.broadcasted_iota(jnp.int32, (BLOCK, 1), 0) < valid

    @pl.when(step == 0)
    def _():
        for block in range(2):
            here = device * 2 + block
            query = lax.broadcasted_iota(jnp.int32, (BLOCK, BLOCK), 0)
            key = lax.broadcasted_iota(jnp.int32, (BLOCK, BLOCK), 1)
            row_ok = here * BLOCK + query < valid
            for piece in range(pieces):
                there = here if piece == 0 else here - 2 ** (piece - 1)
                allowed = row_ok & (there * BLOCK + key < valid)
                if piece == 0:
                    allowed = allowed & (key <= query)
                else:
                    entry = kb[block, piece - 1]
                    allowed = allowed & ((entry >= 0) & (entry == there))
                bias_ref[block, :, piece * BLOCK : (piece + 1) * BLOCK] = jnp.where(
                    allowed, 0.0, -FAR
                )
            level = lax.broadcasted_iota(jnp.int32, (LEVELS, BLOCK), 0)
            row = lax.broadcasted_iota(jnp.int32, (LEVELS, BLOCK), 1)
            flags = jnp.zeros((LEVELS, BLOCK), jnp.float32)
            for index in range(LEVELS):
                entry = kb[block, index]
                hit = ((entry >= 0) & (entry == here - 2**index)).astype(jnp.float32)
                flags = jnp.where(level == index, hit, flags)
            flags = jnp.where(here * BLOCK + row < valid, flags, 0.0)
            stat_ref[stat_ref.shape[0] - 1, :, block * BLOCK : (block + 1) * BLOCK] = flags

    lane = lax.broadcasted_iota(jnp.int32, (BLOCK, BLOCK), 1)
    for head in range(HEADS_STEP):
        query, key, value, grad = (
            head_columns(ref, head) for ref in (q_ref[...], k_ref[...], v_ref[...], g_ref[...])
        )
        far = [head_columns(ref[...], head) for ref in behind]
        for block in range(2):

            def stack(own, which):
                parts = [block_rows(own, block)]
                parts.append(block_rows(far[0], which * 2 + 1) if block == 0 else block_rows(own, 0))
                parts += [block_rows(piece, which * 2 + block) for piece in far]
                return jnp.concatenate(parts, axis=0)

            key_rows, value_rows = stack(key, 0), stack(value, 1)
            query_here, grad_here = block_rows(query, block), block_rows(grad, block)
            scores = product_rows(query_here, key_rows) * SCALE2 + bias_ref[block]
            row_max = jnp.max(scores, axis=1, keepdims=True)
            raw = jnp.exp2(scores - row_max)
            total = jnp.sum(raw, axis=1, keepdims=True)
            inverse = jnp.where(rows_ok(block), 1.0 / total, 0.0)
            weights = raw * inverse
            attended = product(weights.astype(jnp.bfloat16), value_rows).astype(jnp.bfloat16)
            delta = jnp.sum(
                grad_here.astype(jnp.float32) * attended.astype(jnp.float32), axis=1, keepdims=True
            )
            weight_grad = product_rows(grad_here, value_rows)
            score_grad = (weights * (weight_grad - delta)).astype(jnp.bfloat16)
            query_grad = (product(score_grad, key_rows) * SCALE).astype(jnp.bfloat16)
            rows = slice(block * BLOCK, (block + 1) * BLOCK)
            columns = slice(head * HEAD_DIM, (head + 1) * HEAD_DIM)
            att_ref[rows, columns] = attended
            dq_ref[rows, columns] = query_grad
            top = jnp.where(rows_ok(block), row_max, FAR)
            packed = jnp.where(lane == 0, top, jnp.where(lane == 1, inverse, delta))
            stat_ref[step * HEADS_STEP + head, :, rows] = packed.T[:8]


def key_kernel(hops, fresh, info, q_ref, k_ref, v_ref, g_ref, *refs):
    count = len(hops)
    ahead = refs[:count]
    stats = refs[count : 2 * count + 1]
    dk_ref, dv_ref = refs[-2:]
    step = pl.program_id(0)
    device, valid, devices = info[0], info[1], info[2]
    flags = [ref[ref.shape[0] - 1] for ref in stats]
    for head in range(HEADS_STEP):
        query, key, value, grad = (
            head_columns(ref, head) for ref in (q_ref[...], k_ref[...], v_ref[...], g_ref[...])
        )
        far = [head_columns(ref[...], head) for ref in ahead]
        stat = [ref[step * HEADS_STEP + head] for ref in stats]
        for block in range(2):

            def stack(own, which):
                parts = [block_rows(own, block)]
                parts.append(block_rows(own, 1) if block == 0 else block_rows(far[0], which * 2))
                parts += [block_rows(piece, which * 2 + block) for piece in far]
                return jnp.concatenate(parts, axis=0)

            def lanes(array, row, index):
                return array[row : row + 1, index * BLOCK : (index + 1) * BLOCK]

            sources = [(0, block, None)]
            sources.append((0, 1, 0) if block == 0 else (1, 0, 0))
            sources += [(1 + index, block, index + 1) for index in range(count)]
            row_max, inverse, delta = [], [], []
            for source, at, level in sources:
                top = lanes(stat[source], 0, at)
                if level is not None:
                    flag = lanes(flags[source], level, at)
                    if source > 0:
                        flag = jnp.where(device + hops[source - 1] < devices, flag, 0.0)
                    top = jnp.where(flag > 0.5, top, FAR)
                row_max.append(top)
                inverse.append(lanes(stat[source], 1, at))
                delta.append(lanes(stat[source], 2, at))
            row_max, inverse, delta = (
                jnp.concatenate(parts, axis=1) for parts in (row_max, inverse, delta)
            )
            query_rows, grad_rows = stack(query, 0), stack(grad, 1)
            key_here, value_here = block_rows(key, block), block_rows(value, block)
            scores = product_rows(key_here, query_rows) * SCALE2 - row_max
            key_index = lax.broadcasted_iota(jnp.int32, (BLOCK, BLOCK), 0)
            query_index = lax.broadcasted_iota(jnp.int32, (BLOCK, BLOCK), 1)
            causal = jnp.where(key_index <= query_index, scores[:, :BLOCK], -FAR)
            scores = jnp.concatenate([causal, scores[:, BLOCK:]], axis=1)
            weights = jnp.exp2(scores) * inverse
            value_grad = product(weights.astype(jnp.bfloat16), grad_rows)
            weight_grad = product_rows(value_here, grad_rows)
            score_grad = (weights * (weight_grad - delta)).astype(jnp.bfloat16)
            key_grad = product(score_grad, query_rows) * SCALE
            at = (device * 2 + block) * BLOCK
            key_ok = at + lax.broadcasted_iota(jnp.int32, (BLOCK, 1), 0) < valid
            rows = slice(block * BLOCK, (block + 1) * BLOCK)
            columns = slice(head * HEAD_DIM, (head + 1) * HEAD_DIM)
            dk_ref[rows, columns] = jnp.where(key_ok, key_grad, 0.0).astype(jnp.bfloat16)
            dv_ref[rows, columns] = jnp.where(key_ok, value_grad, 0.0).astype(jnp.bfloat16)


def call(kernel, chunk, heads, scalars, own, others, whole, previous, out_shapes, scratch, flops):
    steps = heads // HEADS_STEP
    width = HEADS_STEP * HEAD_DIM
    first = chunk * steps

    def shifted(rows):
        return pl.BlockSpec((rows, width), lambda h: (0, first + h))

    def plain(rows):
        return pl.BlockSpec((rows, width), lambda h: (0, h))

    def entire(array):
        return pl.BlockSpec(array.shape, lambda h: (0,) * len(array.shape))

    in_specs = [pl.BlockSpec(memory_space=pltpu.SMEM) for _ in scalars]
    in_specs += [shifted(array.shape[0]) for array in own]
    operands = list(scalars) + list(own)
    for array, index in others:
        in_specs.append(
            pl.BlockSpec((own[0].shape[0] * 2, width), functools.partial(lambda i, h: (i, h), index))
        )
        operands.append(array)
    for array in whole:
        in_specs.append(entire(array))
        operands.append(array)
    aliases = {}
    for index, array in enumerate(previous):
        aliases[len(operands)] = index
        in_specs.append(pl.BlockSpec(memory_space=pl.ANY))
        operands.append(array)
    out_specs = [shifted(shape.shape[0]) for shape in out_shapes[:2]]
    out_specs += [entire(shape) for shape in out_shapes[2:]]
    return pl.pallas_call(
        kernel,
        grid=(steps,),
        in_specs=in_specs,
        out_specs=out_specs,
        out_shape=out_shapes,
        scratch_shapes=scratch,
        input_output_aliases=aliases,
        cost_estimate=pl.CostEstimate(flops=flops, bytes_accessed=6 << 20, transcendentals=0),
        compiler_params=pltpu.CompilerParams(
            dimension_semantics=("arbitrary",), vmem_limit_bytes=48 << 20
        ),
    )(*operands)


def local(queries, keys, values, out_grad, key_blocks, path_length):
    rows_dev, columns = queries.shape
    head_count = columns // HEAD_DIM
    devices = lax.axis_size("ctx")
    device = lax.axis_index("ctx")
    side, core = (device // 2) % 2, device % 2
    hops = [2**level for level in range(LEVELS - 1) if 2**level < devices]
    info = jnp.stack([device, path_length[0], jnp.int32(devices)]).astype(jnp.int32)

    def up(value, steps):
        return lax.ppermute(value, "ctx", [(at, at + steps) for at in range(devices - steps)])

    def down(value, steps):
        return lax.ppermute(value, "ctx", [(at + steps, at) for at in range(devices - steps)])

    def swap(value, bit):
        return lax.ppermute(value, "ctx", [(at, at ^ bit) for at in range(devices)])

    def back_round(value, steps):
        return lax.ppermute(value, "ctx", [((at + steps) % devices, at) for at in range(devices)])

    heads = head_count // CHUNKS
    width = heads * HEAD_DIM
    packs = []
    for chunk in range(CHUNKS):
        cut = slice(chunk * width, (chunk + 1) * width)
        packs.append(
            (
                jnp.concatenate([keys[:, cut], values[:, cut]], axis=0),
                jnp.concatenate([queries[:, cut], out_grad[:, cut]], axis=0),
            )
        )
    first = []
    for key_pack, query_pack in packs:
        first.append(
            (
                up(key_pack, 4),
                down(query_pack, 4),
                swap(jnp.where(side == 0, key_pack, query_pack), 2),
            )
        )
    moved = []
    for (key_pack, query_pack), stage in zip(packs, first):
        key_4, query_4, side_1 = lax.optimization_barrier(stage)
        side_2 = swap(jnp.where(side == 0, query_4, key_4), 2)
        keys_by, queries_by = {4: key_4}, {4: query_4}
        steps = 4
        while steps * 2 < devices:
            keys_by[steps * 2] = up(keys_by[steps], steps)
            queries_by[steps * 2] = down(queries_by[steps], steps)
            steps *= 2
        side_2, keys_by[8], queries_by[8] = lax.optimization_barrier((side_2, keys_by[8], queries_by[8]))
        keys_by[2] = jnp.where(side == 0, side_2, side_1)
        queries_by[2] = jnp.where(side == 0, side_1, side_2)
        neighbour = swap(
            jnp.concatenate(
                [
                    jnp.where(core == 0, key_pack, keys_by[2]),
                    jnp.where(core == 0, queries_by[2], query_pack),
                ],
                axis=0,
            ),
            1,
        )
        moved.append(
            (
                [(neighbour, 0)] + [(keys_by[hop], 0) for hop in hops[1:]],
                [(neighbour, 1)] + [(queries_by[hop], 0) for hop in hops[1:]],
            )
        )
    own = (queries, keys, values, out_grad)
    full = jax.ShapeDtypeStruct((rows_dev, columns), jnp.bfloat16)
    stat_shape = jax.ShapeDtypeStruct((heads + 1, 8, rows_dev), jnp.float32)
    pieces = 2 + len(hops)
    flops = heads * 2 * pieces * 4 * 2 * BLOCK**3
    front, stats = (), []
    for chunk in range(CHUNKS):
        fresh = chunk == 0
        att, dq, stat = call(
            functools.partial(query_kernel, hops, fresh),
            chunk,
            heads,
            (info, key_blocks),
            own,
            moved[chunk][0],
            (),
            front,
            (full, full, stat_shape),
            [pltpu.VMEM((2, BLOCK, pieces * BLOCK), jnp.float32)],
            flops,
        )
        front = (att, dq)
        stats.append([stat] + [back_round(stat, hop) for hop in hops])
    back = ()
    for chunk in range(CHUNKS):
        back = call(
            functools.partial(key_kernel, hops, chunk == 0),
            chunk,
            heads,
            (info,),
            own,
            moved[chunk][1],
            stats[chunk],
            back,
            (full, full),
            [],
            flops,
        )
    return (front[0], front[1], back[0], back[1])


def solution(mesh):
    placed = (P(("grp", "ctx"), None),) * 5 + (P("grp"),)
    return jax.shard_map(
        local,
        mesh=mesh,
        in_specs=placed,
        out_specs=(P(("grp", "ctx"), None),) * 4,
        check_vma=False,
    )
```

```python
import functools
import math

import jax
import jax.numpy as jnp
from jax import lax
from jax.experimental import pallas as pl
from jax.experimental.pallas import tpu as pltpu
from jax.sharding import PartitionSpec as P

HEAD_DIM = 128
BLOCK = 128
LEVELS = 8
CHUNKS = 2
HEADS_STEP = 4
QUERY_LAG = (0, 1, 2, 3)
KEY_LAG = (0, 1, 1)
FAR = 1e30
SCALE = HEAD_DIM ** (-0.5)
SCALE2 = SCALE * math.log2(math.e)


def product_rows(left, right):
    return lax.dot_general(
        left, right, (((1,), (1,)), ((), ())), preferred_element_type=jnp.float32
    )


def product(left, right):
    return jnp.dot(left, right, preferred_element_type=jnp.float32)


def staged(units, stages, lags):
    for turn in range(len(units) + max(lags)):
        for stage, lag in zip(stages, lags):
            if 0 <= turn - lag < len(units):
                stage(units[turn - lag])


def query_kernel(hops, fresh, info, kb, q_ref, k_ref, v_ref, g_ref, *refs):
    behind = refs[: len(hops)]
    att_ref, dq_ref, stat_ref, bias_ref = refs[-4:]
    step = pl.program_id(0)
    device, valid = info[0], info[1]
    pieces = 2 + len(hops)

    def rows_ok(block):
        at = (device * 2 + block) * BLOCK
        return at + lax.broadcasted_iota(jnp.int32, (BLOCK, 1), 0) < valid

    @pl.when(step == 0)
    def _():
        for block in range(2):
            here = device * 2 + block
            query = lax.broadcasted_iota(jnp.int32, (BLOCK, BLOCK), 0)
            key = lax.broadcasted_iota(jnp.int32, (BLOCK, BLOCK), 1)
            row_ok = here * BLOCK + query < valid
            for piece in range(pieces):
                there = here if piece == 0 else here - 2 ** (piece - 1)
                allowed = row_ok & (there * BLOCK + key < valid)
                if piece == 0:
                    allowed = allowed & (key <= query)
                else:
                    entry = kb[block, piece - 1]
                    allowed = allowed & ((entry >= 0) & (entry == there))
                bias_ref[block, :, piece * BLOCK : (piece + 1) * BLOCK] = jnp.where(
                    allowed, 0.0, -FAR
                )
            level = lax.broadcasted_iota(jnp.int32, (LEVELS, BLOCK), 0)
            row = lax.broadcasted_iota(jnp.int32, (LEVELS, BLOCK), 1)
            flags = jnp.zeros((LEVELS, BLOCK), jnp.float32)
            for index in range(LEVELS):
                entry = kb[block, index]
                hit = ((entry >= 0) & (entry == here - 2**index)).astype(jnp.float32)
                flags = jnp.where(level == index, hit, flags)
            flags = jnp.where(here * BLOCK + row < valid, flags, 0.0)
            stat_ref[stat_ref.shape[0] - 1, :, block * BLOCK : (block + 1) * BLOCK] = flags

    lane = lax.broadcasted_iota(jnp.int32, (BLOCK, BLOCK), 1)
    units = [(head, block) for head in range(HEADS_STEP) for block in range(2)]
    held = {}

    def stack(unit, own_ref, which):
        head, block = unit
        columns = slice(head * HEAD_DIM, (head + 1) * HEAD_DIM)

        def part(ref, index):
            return ref[index * BLOCK : (index + 1) * BLOCK, columns]

        parts = [part(own_ref, block)]
        parts.append(part(behind[0], which * 2 + 1) if block == 0 else part(own_ref, 0))
        parts += [part(ref, which * 2 + block) for ref in behind]
        return jnp.concatenate(parts, axis=0)

    def place(unit):
        head, block = unit
        return (
            slice(block * BLOCK, (block + 1) * BLOCK),
            slice(head * HEAD_DIM, (head + 1) * HEAD_DIM),
        )

    def products(unit):
        rows, columns = place(unit)
        scores = product_rows(q_ref[rows, columns], stack(unit, k_ref, 0))
        weight_grad = product_rows(g_ref[rows, columns], stack(unit, v_ref, 1))
        held[unit] = (scores, weight_grad)

    def soften(unit):
        scores, weight_grad = held[unit]
        scores = scores * SCALE2 + bias_ref[unit[1]]
        row_max = jnp.max(scores, axis=1, keepdims=True)
        raw = jnp.exp2(scores - row_max)
        total = jnp.sum(raw, axis=1, keepdims=True)
        inverse = jnp.where(rows_ok(unit[1]), 1.0 / total, 0.0)
        weights = raw * inverse
        held[unit] = (weights, weight_grad, row_max, inverse)

    def attend(unit):
        weights, weight_grad, row_max, inverse = held[unit]
        rows, columns = place(unit)
        attended = product(weights.astype(jnp.bfloat16), stack(unit, v_ref, 1)).astype(jnp.bfloat16)
        grad_here = g_ref[rows, columns]
        delta = jnp.sum(
            grad_here.astype(jnp.float32) * attended.astype(jnp.float32), axis=1, keepdims=True
        )
        att_ref[rows, columns] = attended
        top = jnp.where(rows_ok(unit[1]), row_max, FAR)
        packed = jnp.where(lane == 0, top, jnp.where(lane == 1, inverse, delta))
        stat_ref[step * HEADS_STEP + unit[0], :, rows] = packed.T[:8]
        held[unit] = (weights, weight_grad, delta)

    def finish(unit):
        weights, weight_grad, delta = held[unit]
        rows, columns = place(unit)
        score_grad = (weights * (weight_grad - delta)).astype(jnp.bfloat16)
        dq_ref[rows, columns] = (product(score_grad, stack(unit, k_ref, 0)) * SCALE).astype(
            jnp.bfloat16
        )

    staged(units, (products, soften, attend, finish), QUERY_LAG)


def key_kernel(hops, fresh, info, q_ref, k_ref, v_ref, g_ref, *refs):
    count = len(hops)
    ahead = refs[:count]
    stats = refs[count : 2 * count + 1]
    dk_ref, dv_ref = refs[-2:]
    step = pl.program_id(0)
    device, valid, devices = info[0], info[1], info[2]
    flags = [ref[ref.shape[0] - 1] for ref in stats]
    units = [(head, block) for head in range(HEADS_STEP) for block in range(2)]
    held = {}

    def stack(unit, own_ref, which):
        head, block = unit
        columns = slice(head * HEAD_DIM, (head + 1) * HEAD_DIM)

        def part(ref, index):
            return ref[index * BLOCK : (index + 1) * BLOCK, columns]

        parts = [part(own_ref, block)]
        parts.append(part(own_ref, 1) if block == 0 else part(ahead[0], which * 2))
        parts += [part(ref, which * 2 + block) for ref in ahead]
        return jnp.concatenate(parts, axis=0)

    def place(unit):
        head, block = unit
        return (
            slice(block * BLOCK, (block + 1) * BLOCK),
            slice(head * HEAD_DIM, (head + 1) * HEAD_DIM),
        )

    def lanes(array, row, index):
        return array[row : row + 1, index * BLOCK : (index + 1) * BLOCK]

    def products(unit):
        rows, columns = place(unit)
        scores = product_rows(k_ref[rows, columns], stack(unit, q_ref, 0))
        weight_grad = product_rows(v_ref[rows, columns], stack(unit, g_ref, 1))
        held[unit] = (scores, weight_grad)

    def soften(unit):
        head, block = unit
        scores, weight_grad = held[unit]
        stat = [ref[step * HEADS_STEP + head] for ref in stats]
        sources = [(0, block, None)]
        sources.append((0, 1, 0) if block == 0 else (1, 0, 0))
        sources += [(1 + index, block, index + 1) for index in range(count)]
        row_max, inverse, delta = [], [], []
        for source, at, level in sources:
            top = lanes(stat[source], 0, at)
            if level is not None:
                flag = lanes(flags[source], level, at)
                if source > 0:
                    flag = jnp.where(device + hops[source - 1] < devices, flag, 0.0)
                top = jnp.where(flag > 0.5, top, FAR)
            row_max.append(top)
            inverse.append(lanes(stat[source], 1, at))
            delta.append(lanes(stat[source], 2, at))
        row_max, inverse, delta = (
            jnp.concatenate(parts, axis=1) for parts in (row_max, inverse, delta)
        )
        scores = scores * SCALE2 - row_max
        key_index = lax.broadcasted_iota(jnp.int32, (BLOCK, BLOCK), 0)
        query_index = lax.broadcasted_iota(jnp.int32, (BLOCK, BLOCK), 1)
        causal = jnp.where(key_index <= query_index, scores[:, :BLOCK], -FAR)
        scores = jnp.concatenate([causal, scores[:, BLOCK:]], axis=1)
        weights = jnp.exp2(scores) * inverse
        score_grad = (weights * (weight_grad - delta)).astype(jnp.bfloat16)
        held[unit] = (weights.astype(jnp.bfloat16), score_grad)

    def finish(unit):
        weights_low, score_grad = held[unit]
        rows, columns = place(unit)
        value_grad = product(weights_low, stack(unit, g_ref, 1))
        key_grad = product(score_grad, stack(unit, q_ref, 0)) * SCALE
        at = (device * 2 + unit[1]) * BLOCK
        key_ok = at + lax.broadcasted_iota(jnp.int32, (BLOCK, 1), 0) < valid
        dk_ref[rows, columns] = jnp.where(key_ok, key_grad, 0.0).astype(jnp.bfloat16)
        dv_ref[rows, columns] = jnp.where(key_ok, value_grad, 0.0).astype(jnp.bfloat16)

    staged(units, (products, soften, finish), KEY_LAG)


def call(kernel, chunk, heads, scalars, own, others, whole, previous, out_shapes, scratch, flops):
    steps = heads // HEADS_STEP
    width = HEADS_STEP * HEAD_DIM
    first = chunk * steps

    def shifted(rows):
        return pl.BlockSpec((rows, width), lambda h: (0, first + h))

    def plain(rows):
        return pl.BlockSpec((rows, width), lambda h: (0, h))

    def entire(array):
        return pl.BlockSpec(array.shape, lambda h: (0,) * len(array.shape))

    in_specs = [pl.BlockSpec(memory_space=pltpu.SMEM) for _ in scalars]
    in_specs += [shifted(array.shape[0]) for array in own]
    operands = list(scalars) + list(own)
    for array, index in others:
        in_specs.append(
            pl.BlockSpec((own[0].shape[0] * 2, width), functools.partial(lambda i, h: (i, h), index))
        )
        operands.append(array)
    for array in whole:
        in_specs.append(entire(array))
        operands.append(array)
    aliases = {}
    for index, array in enumerate(previous):
        aliases[len(operands)] = index
        in_specs.append(pl.BlockSpec(memory_space=pl.ANY))
        operands.append(array)
    out_specs = [shifted(shape.shape[0]) for shape in out_shapes[:2]]
    out_specs += [entire(shape) for shape in out_shapes[2:]]
    return pl.pallas_call(
        kernel,
        grid=(steps,),
        in_specs=in_specs,
        out_specs=out_specs,
        out_shape=out_shapes,
        scratch_shapes=scratch,
        input_output_aliases=aliases,
        cost_estimate=pl.CostEstimate(flops=flops, bytes_accessed=6 << 20, transcendentals=0),
        compiler_params=pltpu.CompilerParams(
            dimension_semantics=("arbitrary",), vmem_limit_bytes=48 << 20
        ),
    )(*operands)


def local(queries, keys, values, out_grad, key_blocks, path_length):
    rows_dev, columns = queries.shape
    head_count = columns // HEAD_DIM
    devices = lax.axis_size("ctx")
    device = lax.axis_index("ctx")
    side, core = (device // 2) % 2, device % 2
    hops = [2**level for level in range(LEVELS - 1) if 2**level < devices]
    info = jnp.stack([device, path_length[0], jnp.int32(devices)]).astype(jnp.int32)

    def up(value, steps):
        return lax.ppermute(value, "ctx", [(at, at + steps) for at in range(devices - steps)])

    def down(value, steps):
        return lax.ppermute(value, "ctx", [(at + steps, at) for at in range(devices - steps)])

    def swap(value, bit):
        return lax.ppermute(value, "ctx", [(at, at ^ bit) for at in range(devices)])

    def back_round(value, steps):
        return lax.ppermute(value, "ctx", [((at + steps) % devices, at) for at in range(devices)])

    heads = head_count // CHUNKS
    width = heads * HEAD_DIM
    packs = []
    for chunk in range(CHUNKS):
        cut = slice(chunk * width, (chunk + 1) * width)
        packs.append(
            (
                jnp.concatenate([keys[:, cut], values[:, cut]], axis=0),
                jnp.concatenate([queries[:, cut], out_grad[:, cut]], axis=0),
            )
        )
    first = []
    for key_pack, query_pack in packs:
        first.append(
            (
                up(key_pack, 4),
                down(query_pack, 4),
                swap(jnp.where(side == 0, key_pack, query_pack), 2),
            )
        )
    own = (queries, keys, values, out_grad)
    full = jax.ShapeDtypeStruct((rows_dev, columns), jnp.bfloat16)
    stat_shape = jax.ShapeDtypeStruct((heads + 1, 8, rows_dev), jnp.float32)
    pieces = 2 + len(hops)
    flops = heads * 2 * pieces * 4 * 2 * BLOCK**3

    middle = []
    for (key_pack, query_pack), stage in zip(packs, first):
        key_4, query_4, side_1 = lax.optimization_barrier(stage)
        side_2 = swap(jnp.where(side == 0, query_4, key_4), 2)
        keys_by, queries_by = {4: key_4}, {4: query_4}
        steps = 4
        while steps * 2 < devices:
            keys_by[steps * 2] = up(keys_by[steps], steps)
            queries_by[steps * 2] = down(queries_by[steps], steps)
            steps *= 2
        middle.append((side_1, side_2, keys_by, queries_by))

    front, stats, moved = (), [], []
    for chunk in range(CHUNKS):
        (key_pack, query_pack), (side_1, side_2, keys_by, queries_by) = packs[chunk], middle[chunk]
        side_2, keys_by[8], queries_by[8] = lax.optimization_barrier((side_2, keys_by[8], queries_by[8]))
        keys_by[2] = jnp.where(side == 0, side_2, side_1)
        queries_by[2] = jnp.where(side == 0, side_1, side_2)
        neighbour = swap(
            jnp.concatenate(
                [
                    jnp.where(core == 0, key_pack, keys_by[2]),
                    jnp.where(core == 0, queries_by[2], query_pack),
                ],
                axis=0,
            ),
            1,
        )
        moved.append(
            (
                [(neighbour, 0)] + [(keys_by[hop], 0) for hop in hops[1:]],
                [(neighbour, 1)] + [(queries_by[hop], 0) for hop in hops[1:]],
            )
        )
        att, dq, stat = call(
            functools.partial(query_kernel, hops, chunk == 0),
            chunk,
            heads,
            (info, key_blocks),
            own,
            moved[chunk][0],
            (),
            front,
            (full, full, stat_shape),
            [pltpu.VMEM((2, BLOCK, pieces * BLOCK), jnp.float32)],
            flops,
        )
        front = (att, dq)
        stats.append([stat] + [back_round(stat, hop) for hop in hops])
    back = ()
    for chunk in range(CHUNKS):
        back = call(
            functools.partial(key_kernel, hops, chunk == 0),
            chunk,
            heads,
            (info,),
            own,
            moved[chunk][1],
            stats[chunk],
            back,
            (full, full),
            [],
            flops,
        )
    return (front[0], front[1], back[0], back[1])


def solution(mesh):
    placed = (P(("grp", "ctx"), None),) * 5 + (P("grp"),)
    return jax.shard_map(
        local,
        mesh=mesh,
        in_specs=placed,
        out_specs=(P(("grp", "ctx"), None),) * 4,
        check_vma=False,
    )
```

```python
import functools
import math

import jax
import jax.numpy as jnp
from jax import lax
from jax.experimental import pallas as pl
from jax.experimental.pallas import tpu as pltpu
from jax.sharding import PartitionSpec as P

HEAD_DIM = 128
BLOCK = 128
LEVELS = 8
CHUNKS = 2
QUERY_LAG = (0, 1, 2, 3)
KEY_LAG = (0, 1, 1)
FAR = 1e30
SCALE = HEAD_DIM ** (-0.5)
SCALE2 = SCALE * math.log2(math.e)


def product_rows(left, right):
    return lax.dot_general(
        left, right, (((1,), (1,)), ((), ())), preferred_element_type=jnp.float32
    )


def product(left, right):
    return jnp.dot(left, right, preferred_element_type=jnp.float32)


def two_heads(left):
    first, second = left[:, :HEAD_DIM], left[:, HEAD_DIM:]
    empty = jnp.zeros_like(first)
    return jnp.concatenate(
        [
            jnp.concatenate([first, empty], axis=1),
            jnp.concatenate([empty, second], axis=1),
        ],
        axis=0,
    )


def pair_rows(left, right):
    both = product_rows(two_heads(left), right)
    return [both[:BLOCK], both[BLOCK:]]


def pair_product(left, right):
    both = product(jnp.concatenate(left, axis=0), right)
    return [both[:BLOCK, :HEAD_DIM], both[BLOCK:, HEAD_DIM:]]


def staged(units, stages, lags):
    for turn in range(len(units) + max(lags)):
        for stage, lag in zip(stages, lags):
            if 0 <= turn - lag < len(units):
                stage(units[turn - lag])


def send_head(copies, head, first, pairs, sems):
    for index, (source, target) in enumerate(pairs):
        copy = pltpu.make_async_copy(
            source.at[:, pl.ds(head * HEAD_DIM, HEAD_DIM)],
            target.at[:, pl.ds((first + head) * HEAD_DIM, HEAD_DIM)],
            sems.at[index, head],
        )
        copy.start()
        copies.append(copy)


def query_kernel(hops, first, info, kb, q_ref, k_ref, v_ref, g_ref, *refs):
    behind = refs[: len(hops) + (first > 0)]
    att_out, dq_out, stat_ref, att_ref, dq_ref, sems, bias_ref = refs[-7:]
    heads = att_ref.shape[1] // HEAD_DIM
    base = first
    device, valid = info[0], info[1]
    pieces = 2 + len(hops)

    def rows_ok(block):
        at = (device * 2 + block) * BLOCK
        return at + lax.broadcasted_iota(jnp.int32, (BLOCK, 1), 0) < valid

    if True:
        for block in range(2):
            here = device * 2 + block
            query = lax.broadcasted_iota(jnp.int32, (BLOCK, BLOCK), 0)
            key = lax.broadcasted_iota(jnp.int32, (BLOCK, BLOCK), 1)
            row_ok = here * BLOCK + query < valid
            for piece in range(pieces):
                there = here if piece == 0 else here - 2 ** (piece - 1)
                allowed = row_ok & (there * BLOCK + key < valid)
                if piece == 0:
                    allowed = allowed & (key <= query)
                else:
                    entry = kb[block, piece - 1]
                    allowed = allowed & ((entry >= 0) & (entry == there))
                bias_ref[block, :, piece * BLOCK : (piece + 1) * BLOCK] = jnp.where(
                    allowed, 0.0, -FAR
                )
            level = lax.broadcasted_iota(jnp.int32, (LEVELS, BLOCK), 0)
            row = lax.broadcasted_iota(jnp.int32, (LEVELS, BLOCK), 1)
            flags = jnp.zeros((LEVELS, BLOCK), jnp.float32)
            for index in range(LEVELS):
                entry = kb[block, index]
                hit = ((entry >= 0) & (entry == here - 2**index)).astype(jnp.float32)
                flags = jnp.where(level == index, hit, flags)
            flags = jnp.where(here * BLOCK + row < valid, flags, 0.0)
            stat_ref[3, :, block * BLOCK : (block + 1) * BLOCK] = flags
        if first:
            stat_ref[:3] = behind[-1][:3]

    lane = lax.broadcasted_iota(jnp.int32, (BLOCK, BLOCK), 1)
    units = [(pair, block) for pair in range(heads // 2) for block in range(2)]
    held = {}

    def stack(unit, own_ref, which):
        pair, block = unit

        def part(ref, index):
            shift = first * HEAD_DIM if ref is own_ref else 0
            return ref[
                index * BLOCK : (index + 1) * BLOCK, pl.ds(shift + pair * 2 * HEAD_DIM, 2 * HEAD_DIM)
            ]

        parts = [part(own_ref, block)]
        parts.append(part(behind[0], which * 2 + 1) if block == 0 else part(own_ref, 0))
        parts += [part(ref, which * 2 + block) for ref in behind[: len(hops)]]
        return jnp.concatenate(parts, axis=0)

    def place(unit, shift=0):
        pair, block = unit
        return (
            slice(block * BLOCK, (block + 1) * BLOCK),
            slice((shift + 2 * pair) * HEAD_DIM, (shift + 2 * pair + 2) * HEAD_DIM),
        )

    def products(unit):
        rows, columns = place(unit, first)
        scores = pair_rows(q_ref[rows, columns], stack(unit, k_ref, 0))
        weight_grad = pair_rows(g_ref[rows, columns], stack(unit, v_ref, 1))
        held[unit] = (scores, weight_grad)

    def soften(unit):
        both, weight_grad = held[unit]
        weights, top, inverses = [], [], []
        for scores in both:
            scores = scores * SCALE2 + bias_ref[unit[1]]
            row_max = jnp.max(scores, axis=1, keepdims=True)
            raw = jnp.exp2(scores - row_max)
            total = jnp.sum(raw, axis=1, keepdims=True)
            inverse = jnp.where(rows_ok(unit[1]), 1.0 / total, 0.0)
            weights.append(raw * inverse)
            top.append(jnp.where(rows_ok(unit[1]), row_max, FAR))
            inverses.append(inverse)
        held[unit] = (weights, weight_grad, top, inverses)

    def attend(unit):
        weights, weight_grad, top, inverse = held[unit]
        rows, columns = place(unit)
        attended = pair_product([w.astype(jnp.bfloat16) for w in weights], stack(unit, v_ref, 1))
        attended = jnp.concatenate(attended, axis=1).astype(jnp.bfloat16)
        att_ref[rows, columns] = attended
        terms = g_ref[place(unit, first)].astype(jnp.float32) * attended.astype(jnp.float32)
        deltas = []
        for index in range(2):
            delta = jnp.sum(
                terms[:, index * HEAD_DIM : (index + 1) * HEAD_DIM], axis=1, keepdims=True
            )
            packed = jnp.where(lane == 0, top[index], jnp.where(lane == 1, inverse[index], delta))
            turned = packed.T
            for kind in range(3):
                at = base + 2 * unit[0] + index
                stat_ref[kind, at : at + 1, rows] = turned[kind : kind + 1]
            deltas.append(delta)
        held[unit] = (weights, weight_grad, deltas)

    def finish(unit):
        score_grad = [
            (w * (wg - d)).astype(jnp.bfloat16) for w, wg, d in zip(*held[unit])
        ]
        query_grad = pair_product(score_grad, stack(unit, k_ref, 0))
        dq_ref[place(unit)] = (jnp.concatenate(query_grad, axis=1) * SCALE).astype(jnp.bfloat16)
        if unit[1] == 1:
            for head in (2 * unit[0], 2 * unit[0] + 1):
                send_head(copies, head, first, ((att_ref, att_out), (dq_ref, dq_out)), sems)

    copies = []
    staged(units, (products, soften, attend, finish), QUERY_LAG)
    for copy in copies:
        copy.wait()


def key_kernel(hops, chunks, info, q_ref, k_ref, v_ref, g_ref, *refs):
    count = len(hops)
    ahead_all = [refs[chunk * count : (chunk + 1) * count] for chunk in range(chunks)]
    stats = refs[chunks * count : (chunks + 1) * count + 1]
    dk_out, dv_out, dk_ref, dv_ref, sems = refs[-5:]
    heads = dk_ref.shape[1] // HEAD_DIM
    device, valid, devices = info[0], info[1], info[2]
    flags = [ref[3] for ref in stats]
    units = [(pair, block) for pair in range(heads // 2) for block in range(2)]
    held = {}

    def stack(unit, own_ref, which):
        pair, block = unit
        chunk = pair * chunks * 2 // heads
        ahead = ahead_all[chunk]

        def part(ref, index):
            shift = 0 if ref is own_ref else -chunk * heads // chunks * HEAD_DIM
            return ref[
                index * BLOCK : (index + 1) * BLOCK, pl.ds(shift + pair * 2 * HEAD_DIM, 2 * HEAD_DIM)
            ]

        parts = [part(own_ref, block)]
        parts.append(part(own_ref, 1) if block == 0 else part(ahead[0], 4 + which * 2))
        parts += [
            part(ref, which * 2 + block + (4 if index == 0 else 0)) for index, ref in enumerate(ahead)
        ]
        return jnp.concatenate(parts, axis=0)

    def place(unit, shift=0):
        pair, block = unit
        return (
            slice(block * BLOCK, (block + 1) * BLOCK),
            slice((shift + 2 * pair) * HEAD_DIM, (shift + 2 * pair + 2) * HEAD_DIM),
        )

    def lanes(array, row, index):
        return array[row : row + 1, index * BLOCK : (index + 1) * BLOCK]

    def products(unit):
        rows, columns = place(unit)
        scores = pair_rows(k_ref[rows, columns], stack(unit, q_ref, 0))
        weight_grad = pair_rows(v_ref[rows, columns], stack(unit, g_ref, 1))
        held[unit] = (scores, weight_grad)

    def soften(unit):
        pair, block = unit
        held[unit] = [
            soften_head(2 * pair + index, block, held[unit][0][index], held[unit][1][index])
            for index in range(2)
        ]

    def soften_head(head, block, scores, weight_grad):
        stat = [
            [ref[kind, head : head + 1, :] for kind in range(3)] for ref in stats
        ]
        sources = [(0, block, None)]
        sources.append((0, 1, 0) if block == 0 else (1, 0, 0))
        sources += [(1 + index, block, index + 1) for index in range(count)]
        row_max, inverse, delta = [], [], []
        for source, at, level in sources:
            top = lanes(stat[source][0], 0, at)
            if level is not None:
                flag = lanes(flags[source], level, at)
                if source > 0:
                    flag = jnp.where(device + hops[source - 1] < devices, flag, 0.0)
                top = jnp.where(flag > 0.5, top, FAR)
            row_max.append(top)
            inverse.append(lanes(stat[source][1], 0, at))
            delta.append(lanes(stat[source][2], 0, at))
        row_max, inverse, delta = (
            jnp.concatenate(parts, axis=1) for parts in (row_max, inverse, delta)
        )
        scores = scores * SCALE2 - row_max
        key_index = lax.broadcasted_iota(jnp.int32, (BLOCK, BLOCK), 0)
        query_index = lax.broadcasted_iota(jnp.int32, (BLOCK, BLOCK), 1)
        causal = jnp.where(key_index <= query_index, scores[:, :BLOCK], -FAR)
        scores = jnp.concatenate([causal, scores[:, BLOCK:]], axis=1)
        weights = jnp.exp2(scores) * inverse
        score_grad = (weights * (weight_grad - delta)).astype(jnp.bfloat16)
        return (weights.astype(jnp.bfloat16), score_grad)

    def finish(unit):
        weights_low, score_grad = zip(*held[unit])
        rows, columns = place(unit)
        value_grad = jnp.concatenate(pair_product(weights_low, stack(unit, g_ref, 1)), axis=1)
        key_grad = jnp.concatenate(pair_product(score_grad, stack(unit, q_ref, 0)), axis=1) * SCALE
        at = (device * 2 + unit[1]) * BLOCK
        key_ok = at + lax.broadcasted_iota(jnp.int32, (BLOCK, 1), 0) < valid
        dk_ref[rows, columns] = jnp.where(key_ok, key_grad, 0.0).astype(jnp.bfloat16)
        dv_ref[rows, columns] = jnp.where(key_ok, value_grad, 0.0).astype(jnp.bfloat16)
        if unit[1] == 1:
            for head in (2 * unit[0], 2 * unit[0] + 1):
                send_head(copies, head, 0, ((dk_ref, dk_out), (dv_ref, dv_out)), sems)

    copies = []
    staged(units, (products, soften, finish), KEY_LAG)
    for copy in copies:
        copy.wait()


def call(kernel, heads, scalars, arrays, previous, out_shapes, scratch, flops):
    width = heads * HEAD_DIM
    in_specs = [pl.BlockSpec(memory_space=pltpu.SMEM) for _ in scalars]
    in_specs += [pl.BlockSpec(memory_space=pltpu.VMEM) for _ in arrays]
    in_specs += [pl.BlockSpec(memory_space=pl.ANY) for _ in previous]
    before = len(scalars) + len(arrays)
    out_specs = [pl.BlockSpec(memory_space=pl.ANY)] * 2
    out_specs += [pl.BlockSpec(memory_space=pltpu.VMEM)] * (len(out_shapes) - 2)
    rows = out_shapes[0].shape[0]
    return pl.pallas_call(
        kernel,
        in_specs=in_specs,
        out_specs=out_specs,
        out_shape=out_shapes,
        scratch_shapes=[
            pltpu.VMEM((rows, width), jnp.bfloat16),
            pltpu.VMEM((rows, width), jnp.bfloat16),
            pltpu.SemaphoreType.DMA((2, heads)),
        ]
        + scratch,
        input_output_aliases={before + index: index for index in range(len(previous))},
        cost_estimate=pl.CostEstimate(flops=flops, bytes_accessed=6 << 20, transcendentals=0),
        compiler_params=pltpu.CompilerParams(vmem_limit_bytes=24 << 20),
    )(*scalars, *arrays, *previous)


def local(queries, keys, values, out_grad, key_blocks, path_length):
    rows_dev, columns = queries.shape
    head_count = columns // HEAD_DIM
    devices = lax.axis_size("ctx")
    device = lax.axis_index("ctx")
    side, core = (device // 2) % 2, device % 2
    hops = [2**level for level in range(LEVELS - 1) if 2**level < devices]
    info = jnp.stack([device, path_length[0], jnp.int32(devices)]).astype(jnp.int32)

    def up(value, steps):
        return lax.ppermute(value, "ctx", [(at, at + steps) for at in range(devices - steps)])

    def down(value, steps):
        return lax.ppermute(value, "ctx", [(at + steps, at) for at in range(devices - steps)])

    def swap(value, bit):
        return lax.ppermute(value, "ctx", [(at, at ^ bit) for at in range(devices)])

    def back_round(value, steps):
        return lax.ppermute(value, "ctx", [((at + steps) % devices, at) for at in range(devices)])

    heads = head_count // CHUNKS
    width = heads * HEAD_DIM
    packs = []
    for chunk in range(CHUNKS):
        cut = slice(chunk * width, (chunk + 1) * width)
        packs.append(
            (
                jnp.concatenate([keys[:, cut], values[:, cut]], axis=0),
                jnp.concatenate([queries[:, cut], out_grad[:, cut]], axis=0),
            )
        )
    first = []
    for key_pack, query_pack in packs:
        first.append(
            (
                up(key_pack, 4),
                down(query_pack, 4),
                swap(jnp.where(side == 0, key_pack, query_pack), 2),
            )
        )
    own = (queries, keys, values, out_grad)
    full = jax.ShapeDtypeStruct((rows_dev, columns), jnp.bfloat16)
    stat_shape = jax.ShapeDtypeStruct((4, max(head_count, LEVELS), rows_dev), jnp.float32)
    pieces = 2 + len(hops)
    flops = heads * 2 * pieces * 4 * 2 * BLOCK**3

    middle = []
    for (key_pack, query_pack), stage in zip(packs, first):
        key_4, query_4, side_1 = lax.optimization_barrier(stage)
        side_2 = swap(jnp.where(side == 0, query_4, key_4), 2)
        keys_by, queries_by = {4: key_4}, {4: query_4}
        steps = 4
        while steps * 2 < devices:
            keys_by[steps * 2] = up(keys_by[steps], steps)
            queries_by[steps * 2] = down(queries_by[steps], steps)
            steps *= 2
        middle.append((side_1, side_2, keys_by, queries_by))

    front, stats, moved = (), [], []
    for chunk in range(CHUNKS):
        (key_pack, query_pack), (side_1, side_2, keys_by, queries_by) = packs[chunk], middle[chunk]
        side_2, keys_by[8], queries_by[8] = lax.optimization_barrier((side_2, keys_by[8], queries_by[8]))
        keys_by[2] = jnp.where(side == 0, side_2, side_1)
        queries_by[2] = jnp.where(side == 0, side_1, side_2)
        neighbour = swap(
            jnp.concatenate(
                [
                    jnp.where(core == 0, key_pack, keys_by[2]),
                    jnp.where(core == 0, queries_by[2], query_pack),
                ],
                axis=0,
            ),
            1,
        )
        moved.append(
            (
                [neighbour] + [keys_by[hop] for hop in hops[1:]],
                [neighbour] + [queries_by[hop] for hop in hops[1:]],
            )
        )
        att, dq, stat = call(
            functools.partial(query_kernel, hops, chunk * heads),
            heads,
            (info, key_blocks),
            own + tuple(moved[chunk][0]) + tuple(stats[-1:]),
            front,
            (full, full, stat_shape),
            [pltpu.VMEM((2, BLOCK, pieces * BLOCK), jnp.float32)],
            flops,
        )
        front = (att, dq)
        stats.append(stat)
    stats = [stat] + [back_round(stat, hop) for hop in hops]
    back = call(
        functools.partial(key_kernel, hops, CHUNKS),
        head_count,
        (info,),
        own + sum((tuple(pair[1]) for pair in moved), ()) + tuple(stats),
        (),
        (full, full),
        [],
        2 * flops,
    )
    return (front[0], front[1], back[0], back[1])


def solution(mesh):
    placed = (P(("grp", "ctx"), None),) * 5 + (P("grp"),)
    return jax.shard_map(
        local,
        mesh=mesh,
        in_specs=placed,
        out_specs=(P(("grp", "ctx"), None),) * 4,
        check_vma=False,
    )
```

```python
import functools
import math

import jax
import jax.numpy as jnp
from jax import lax
from jax.experimental import pallas as pl
from jax.experimental.pallas import tpu as pltpu
from jax.sharding import PartitionSpec as P

HEAD_DIM = 128
BLOCK = 128
LEVELS = 8
CHUNKS = 2
QUERY_LAG = (0, 1, 2, 3)
KEY_LAG = (0, 1)
FAR = 1e30
SCALE = HEAD_DIM ** (-0.5)
SCALE2 = SCALE * math.log2(math.e)


def product_rows(left, right):
    return lax.dot_general(
        left, right, (((1,), (1,)), ((), ())), preferred_element_type=jnp.float32
    )


def product(left, right):
    return jnp.dot(left, right, preferred_element_type=jnp.float32)


def two_heads(left):
    first, second = left[:, :HEAD_DIM], left[:, HEAD_DIM:]
    empty = jnp.zeros_like(first)
    return jnp.concatenate(
        [
            jnp.concatenate([first, empty], axis=1),
            jnp.concatenate([empty, second], axis=1),
        ],
        axis=0,
    )


def pair_rows(left, right):
    both = product_rows(two_heads(left), right)
    return [both[:BLOCK], both[BLOCK:]]


def pair_product(left, right):
    both = product(jnp.concatenate(left, axis=0), right)
    return [both[:BLOCK, :HEAD_DIM], both[BLOCK:, HEAD_DIM:]]


def staged(units, stages, lags):
    for turn in range(len(units) + max(lags)):
        for stage, lag in zip(stages, lags):
            if 0 <= turn - lag < len(units):
                stage(units[turn - lag])


def send_head(copies, head, first, pairs, sems):
    for index, (source, target) in enumerate(pairs):
        copy = pltpu.make_async_copy(
            source.at[:, pl.ds(head * HEAD_DIM, HEAD_DIM)],
            target.at[:, pl.ds((first + head) * HEAD_DIM, HEAD_DIM)],
            sems.at[index, head],
        )
        copy.start()
        copies.append(copy)


def query_kernel(hops, first, info, kb, q_ref, k_ref, v_ref, g_ref, *refs):
    behind = refs[: len(hops) + (first > 0)]
    att_out, dq_out, stat_ref, att_ref, dq_ref, sems, bias_ref = refs[-7:]
    heads = att_ref.shape[1] // HEAD_DIM
    base = first
    device, valid = info[0], info[1]
    pieces = 2 + len(hops)

    def rows_ok(block):
        at = (device * 2 + block) * BLOCK
        return at + lax.broadcasted_iota(jnp.int32, (BLOCK, 1), 0) < valid

    if True:
        for block in range(2):
            here = device * 2 + block
            query = lax.broadcasted_iota(jnp.int32, (BLOCK, BLOCK), 0)
            key = lax.broadcasted_iota(jnp.int32, (BLOCK, BLOCK), 1)
            row_ok = here * BLOCK + query < valid
            for piece in range(pieces):
                there = here if piece == 0 else here - 2 ** (piece - 1)
                allowed = row_ok & (there * BLOCK + key < valid)
                if piece == 0:
                    allowed = allowed & (key <= query)
                else:
                    entry = kb[block, piece - 1]
                    allowed = allowed & ((entry >= 0) & (entry == there))
                bias_ref[block, :, piece * BLOCK : (piece + 1) * BLOCK] = jnp.where(
                    allowed, 0.0, -FAR
                )
            level = lax.broadcasted_iota(jnp.int32, (LEVELS, BLOCK), 0)
            row = lax.broadcasted_iota(jnp.int32, (LEVELS, BLOCK), 1)
            flags = jnp.zeros((LEVELS, BLOCK), jnp.float32)
            for index in range(LEVELS):
                entry = kb[block, index]
                hit = ((entry >= 0) & (entry == here - 2**index)).astype(jnp.float32)
                flags = jnp.where(level == index, hit, flags)
            flags = jnp.where(here * BLOCK + row < valid, flags, 0.0)
            stat_ref[3, :, block * BLOCK : (block + 1) * BLOCK] = flags
        if first:
            stat_ref[:3] = behind[-1][:3]

    lane = lax.broadcasted_iota(jnp.int32, (BLOCK, BLOCK), 1)
    units = [(pair, block) for pair in range(heads // 2) for block in range(2)]
    held = {}

    def stack(unit, own_ref, which):
        pair, block = unit

        def part(ref, index):
            shift = first * HEAD_DIM if ref is own_ref else 0
            return ref[
                index * BLOCK : (index + 1) * BLOCK, pl.ds(shift + pair * 2 * HEAD_DIM, 2 * HEAD_DIM)
            ]

        parts = [part(own_ref, block)]
        parts.append(part(behind[0], which * 2 + 1) if block == 0 else part(own_ref, 0))
        parts += [part(ref, which * 2 + block) for ref in behind[: len(hops)]]
        return jnp.concatenate(parts, axis=0)

    def place(unit, shift=0):
        pair, block = unit
        return (
            slice(block * BLOCK, (block + 1) * BLOCK),
            slice((shift + 2 * pair) * HEAD_DIM, (shift + 2 * pair + 2) * HEAD_DIM),
        )

    def products(unit):
        rows, columns = place(unit, first)
        scores = pair_rows(q_ref[rows, columns], stack(unit, k_ref, 0))
        weight_grad = pair_rows(g_ref[rows, columns], stack(unit, v_ref, 1))
        held[unit] = (scores, weight_grad)

    def soften(unit):
        both, weight_grad = held[unit]
        weights, top, inverses = [], [], []
        for scores in both:
            scores = scores * SCALE2 + bias_ref[unit[1]]
            row_max = jnp.max(scores, axis=1, keepdims=True)
            raw = jnp.exp2(scores - row_max)
            total = jnp.sum(raw, axis=1, keepdims=True)
            inverse = jnp.where(rows_ok(unit[1]), 1.0 / total, 0.0)
            weights.append(raw * inverse)
            top.append(jnp.where(rows_ok(unit[1]), row_max, FAR))
            inverses.append(inverse)
        held[unit] = (weights, weight_grad, top, inverses)

    def attend(unit):
        weights, weight_grad, top, inverse = held[unit]
        rows, columns = place(unit)
        attended = pair_product([w.astype(jnp.bfloat16) for w in weights], stack(unit, v_ref, 1))
        attended = jnp.concatenate(attended, axis=1).astype(jnp.bfloat16)
        att_ref[rows, columns] = attended
        terms = g_ref[place(unit, first)].astype(jnp.float32) * attended.astype(jnp.float32)
        deltas = []
        for index in range(2):
            delta = jnp.sum(
                terms[:, index * HEAD_DIM : (index + 1) * HEAD_DIM], axis=1, keepdims=True
            )
            packed = jnp.where(lane == 0, top[index], jnp.where(lane == 1, inverse[index], delta))
            turned = packed.T
            for kind in range(3):
                at = base + 2 * unit[0] + index
                stat_ref[kind, at : at + 1, rows] = turned[kind : kind + 1]
            deltas.append(delta)
        held[unit] = (weights, weight_grad, deltas)

    def finish(unit):
        score_grad = [
            (w * (wg - d)).astype(jnp.bfloat16) for w, wg, d in zip(*held[unit])
        ]
        query_grad = pair_product(score_grad, stack(unit, k_ref, 0))
        dq_ref[place(unit)] = (jnp.concatenate(query_grad, axis=1) * SCALE).astype(jnp.bfloat16)
        if unit[1] == 1:
            for head in (2 * unit[0], 2 * unit[0] + 1):
                send_head(copies, head, first, ((att_ref, att_out), (dq_ref, dq_out)), sems)

    copies = []
    staged(units, (products, soften, attend, finish), QUERY_LAG)
    for copy in copies:
        copy.wait()


def key_stack(hops, chunks, heads, refs):
    count = len(hops)

    def stack(unit, own_ref, which):
        pair, block = unit
        chunk = pair * chunks * 2 // heads
        ahead = refs[chunk * count : (chunk + 1) * count]

        def part(ref, index):
            shift = 0 if ref is own_ref else -chunk * heads // chunks * HEAD_DIM
            return ref[
                index * BLOCK : (index + 1) * BLOCK, pl.ds(shift + pair * 2 * HEAD_DIM, 2 * HEAD_DIM)
            ]

        parts = [part(own_ref, block)]
        parts.append(part(own_ref, 1) if block == 0 else part(ahead[0], 4 + which * 2))
        parts += [
            part(ref, which * 2 + block + (4 if index == 0 else 0)) for index, ref in enumerate(ahead)
        ]
        return jnp.concatenate(parts, axis=0)

    return stack


def product_kernel(hops, chunks, q_ref, k_ref, v_ref, g_ref, *refs):
    score_ref, grad_ref = refs[-2:]
    heads = q_ref.shape[1] // HEAD_DIM
    stack = key_stack(hops, chunks, heads, refs)
    for pair in range(heads // 2):
        for block in range(2):
            rows = slice(block * BLOCK, (block + 1) * BLOCK)
            columns = slice(2 * pair * HEAD_DIM, (2 * pair + 2) * HEAD_DIM)
            unit = (pair, block)
            scores = pair_rows(k_ref[rows, columns], stack(unit, q_ref, 0))
            weight_grad = pair_rows(v_ref[rows, columns], stack(unit, g_ref, 1))
            for index in range(2):
                score_ref[2 * pair + index, rows] = scores[index]
                grad_ref[2 * pair + index, rows] = weight_grad[index]


def key_kernel(hops, chunks, info, score_ref, grad_ref, q_ref, g_ref, *refs):
    count = len(hops)
    stats = refs[chunks * count : (chunks + 1) * count + 1]
    dk_out, dv_out, dk_ref, dv_ref, sems = refs[-5:]
    heads = dk_ref.shape[1] // HEAD_DIM
    device, valid, devices = info[0], info[1], info[2]
    flags = [ref[3] for ref in stats]
    units = [(pair, block) for pair in range(heads // 2) for block in range(2)]
    held = {}
    stack = key_stack(hops, chunks, heads, refs)

    def place(unit, shift=0):
        pair, block = unit
        return (
            slice(block * BLOCK, (block + 1) * BLOCK),
            slice((shift + 2 * pair) * HEAD_DIM, (shift + 2 * pair + 2) * HEAD_DIM),
        )

    def lanes(array, row, index):
        return array[row : row + 1, index * BLOCK : (index + 1) * BLOCK]

    def soften(unit):
        pair, block = unit
        held[unit] = [
            soften_head(2 * pair + index, block)
            for index in range(2)
        ]

    def soften_head(head, block):
        scores = score_ref[head, block * BLOCK : (block + 1) * BLOCK]
        weight_grad = grad_ref[head, block * BLOCK : (block + 1) * BLOCK]
        stat = [
            [ref[kind, head : head + 1, :] for kind in range(3)] for ref in stats
        ]
        sources = [(0, block, None)]
        sources.append((0, 1, 0) if block == 0 else (1, 0, 0))
        sources += [(1 + index, block, index + 1) for index in range(count)]
        row_max, inverse, delta = [], [], []
        for source, at, level in sources:
            top = lanes(stat[source][0], 0, at)
            if level is not None:
                flag = lanes(flags[source], level, at)
                if source > 0:
                    flag = jnp.where(device + hops[source - 1] < devices, flag, 0.0)
                top = jnp.where(flag > 0.5, top, FAR)
            row_max.append(top)
            inverse.append(lanes(stat[source][1], 0, at))
            delta.append(lanes(stat[source][2], 0, at))
        row_max, inverse, delta = (
            jnp.concatenate(parts, axis=1) for parts in (row_max, inverse, delta)
        )
        scores = scores * SCALE2 - row_max
        key_index = lax.broadcasted_iota(jnp.int32, (BLOCK, BLOCK), 0)
        query_index = lax.broadcasted_iota(jnp.int32, (BLOCK, BLOCK), 1)
        causal = jnp.where(key_index <= query_index, scores[:, :BLOCK], -FAR)
        scores = jnp.concatenate([causal, scores[:, BLOCK:]], axis=1)
        weights = jnp.exp2(scores) * inverse
        score_grad = (weights * (weight_grad - delta)).astype(jnp.bfloat16)
        return (weights.astype(jnp.bfloat16), score_grad)

    def finish(unit):
        weights_low, score_grad = zip(*held[unit])
        rows, columns = place(unit)
        value_grad = jnp.concatenate(pair_product(weights_low, stack(unit, g_ref, 1)), axis=1)
        key_grad = jnp.concatenate(pair_product(score_grad, stack(unit, q_ref, 0)), axis=1) * SCALE
        at = (device * 2 + unit[1]) * BLOCK
        key_ok = at + lax.broadcasted_iota(jnp.int32, (BLOCK, 1), 0) < valid
        dk_ref[rows, columns] = jnp.where(key_ok, key_grad, 0.0).astype(jnp.bfloat16)
        dv_ref[rows, columns] = jnp.where(key_ok, value_grad, 0.0).astype(jnp.bfloat16)
        if unit[1] == 1:
            for head in (2 * unit[0], 2 * unit[0] + 1):
                send_head(copies, head, 0, ((dk_ref, dk_out), (dv_ref, dv_out)), sems)

    copies = []
    staged(units, (soften, finish), KEY_LAG)
    for copy in copies:
        copy.wait()


def call(kernel, heads, scalars, arrays, previous, out_shapes, scratch, flops):
    width = heads * HEAD_DIM
    in_specs = [pl.BlockSpec(memory_space=pltpu.SMEM) for _ in scalars]
    in_specs += [pl.BlockSpec(memory_space=pltpu.VMEM) for _ in arrays]
    in_specs += [pl.BlockSpec(memory_space=pl.ANY) for _ in previous]
    before = len(scalars) + len(arrays)
    out_specs = [pl.BlockSpec(memory_space=pl.ANY)] * 2
    out_specs += [pl.BlockSpec(memory_space=pltpu.VMEM)] * (len(out_shapes) - 2)
    rows = out_shapes[0].shape[0]
    return pl.pallas_call(
        kernel,
        in_specs=in_specs,
        out_specs=out_specs,
        out_shape=out_shapes,
        scratch_shapes=[
            pltpu.VMEM((rows, width), jnp.bfloat16),
            pltpu.VMEM((rows, width), jnp.bfloat16),
            pltpu.SemaphoreType.DMA((2, heads)),
        ]
        + scratch,
        input_output_aliases={before + index: index for index in range(len(previous))},
        cost_estimate=pl.CostEstimate(flops=flops, bytes_accessed=6 << 20, transcendentals=0),
        compiler_params=pltpu.CompilerParams(vmem_limit_bytes=16 << 20),
    )(*scalars, *arrays, *previous)


def local(queries, keys, values, out_grad, key_blocks, path_length):
    rows_dev, columns = queries.shape
    head_count = columns // HEAD_DIM
    devices = lax.axis_size("ctx")
    device = lax.axis_index("ctx")
    side, core = (device // 2) % 2, device % 2
    hops = [2**level for level in range(LEVELS - 1) if 2**level < devices]
    info = jnp.stack([device, path_length[0], jnp.int32(devices)]).astype(jnp.int32)

    def up(value, steps):
        return lax.ppermute(value, "ctx", [(at, at + steps) for at in range(devices - steps)])

    def down(value, steps):
        return lax.ppermute(value, "ctx", [(at + steps, at) for at in range(devices - steps)])

    def swap(value, bit):
        return lax.ppermute(value, "ctx", [(at, at ^ bit) for at in range(devices)])

    def back_round(value, steps):
        return lax.ppermute(value, "ctx", [((at + steps) % devices, at) for at in range(devices)])

    heads = head_count // CHUNKS
    width = heads * HEAD_DIM
    packs = []
    for chunk in range(CHUNKS):
        cut = slice(chunk * width, (chunk + 1) * width)
        packs.append(
            (
                jnp.concatenate([keys[:, cut], values[:, cut]], axis=0),
                jnp.concatenate([queries[:, cut], out_grad[:, cut]], axis=0),
            )
        )
    first = []
    for key_pack, query_pack in packs:
        first.append(
            (
                up(key_pack, 4),
                down(query_pack, 4),
                swap(jnp.where(side == 0, key_pack, query_pack), 2),
            )
        )
    own = (queries, keys, values, out_grad)
    full = jax.ShapeDtypeStruct((rows_dev, columns), jnp.bfloat16)
    stat_shape = jax.ShapeDtypeStruct((4, max(head_count, LEVELS), rows_dev), jnp.float32)
    pieces = 2 + len(hops)
    flops = heads * 2 * pieces * 4 * 2 * BLOCK**3

    middle = []
    for (key_pack, query_pack), stage in zip(packs, first):
        key_4, query_4, side_1 = lax.optimization_barrier(stage)
        side_2 = swap(jnp.where(side == 0, query_4, key_4), 2)
        keys_by, queries_by = {4: key_4}, {4: query_4}
        steps = 4
        while steps * 2 < devices:
            keys_by[steps * 2] = up(keys_by[steps], steps)
            queries_by[steps * 2] = down(queries_by[steps], steps)
            steps *= 2
        middle.append((side_1, side_2, keys_by, queries_by))

    front, stats, moved = (), [], []
    for chunk in range(CHUNKS):
        (key_pack, query_pack), (side_1, side_2, keys_by, queries_by) = packs[chunk], middle[chunk]
        side_2, keys_by[8], queries_by[8] = lax.optimization_barrier((side_2, keys_by[8], queries_by[8]))
        keys_by[2] = jnp.where(side == 0, side_2, side_1)
        queries_by[2] = jnp.where(side == 0, side_1, side_2)
        neighbour = swap(
            jnp.concatenate(
                [
                    jnp.where(core == 0, key_pack, keys_by[2]),
                    jnp.where(core == 0, queries_by[2], query_pack),
                ],
                axis=0,
            ),
            1,
        )
        moved.append(
            (
                [neighbour] + [keys_by[hop] for hop in hops[1:]],
                [neighbour] + [queries_by[hop] for hop in hops[1:]],
            )
        )
        att, dq, stat = call(
            functools.partial(query_kernel, hops, chunk * heads),
            heads,
            (info, key_blocks),
            own + tuple(moved[chunk][0]) + tuple(stats[-1:]),
            front,
            (full, full, stat_shape),
            [pltpu.VMEM((2, BLOCK, pieces * BLOCK), jnp.float32)],
            flops,
        )
        front = (att, dq)
        stats.append(stat)
    stats = [stat] + [back_round(stat, hop) for hop in hops]
    ahead = sum((tuple(pair[1]) for pair in moved), ())
    raw_shape = jax.ShapeDtypeStruct((head_count, rows_dev, pieces * BLOCK), jnp.float32)
    raw = pl.pallas_call(
        functools.partial(product_kernel, hops, CHUNKS),
        in_specs=[pl.BlockSpec(memory_space=pltpu.VMEM)] * (len(own) + len(ahead)),
        out_specs=[pl.BlockSpec(memory_space=pltpu.VMEM)] * 2,
        out_shape=(raw_shape, raw_shape),
        cost_estimate=pl.CostEstimate(flops=2 * flops, bytes_accessed=6 << 20, transcendentals=0),
        compiler_params=pltpu.CompilerParams(vmem_limit_bytes=16 << 20),
    )(*own, *ahead)
    back = call(
        functools.partial(key_kernel, hops, CHUNKS),
        head_count,
        (info,),
        tuple(raw) + (queries, out_grad) + ahead + tuple(stats),
        (),
        (full, full),
        [],
        2 * flops,
    )
    return (front[0], front[1], back[0], back[1])


def solution(mesh):
    placed = (P(("grp", "ctx"), None),) * 5 + (P("grp"),)
    return jax.shard_map(
        local,
        mesh=mesh,
        in_specs=placed,
        out_specs=(P(("grp", "ctx"), None),) * 4,
        check_vma=False,
    )
```

```python
import functools
import math

import jax
import jax.numpy as jnp
from jax import lax
from jax.experimental import pallas as pl
from jax.experimental.pallas import tpu as pltpu
from jax.sharding import PartitionSpec as P

HEAD_DIM = 128
BLOCK = 128
LEVELS = 8
CHUNKS = 2
QUERY_LAG = (0, 1, 2, 3)
KEY_LAG = (0, 1)
FAR = 1e30
SCALE = HEAD_DIM ** (-0.5)
SCALE2 = SCALE * math.log2(math.e)


def product_rows(left, right):
    return lax.dot_general(
        left, right, (((1,), (1,)), ((), ())), preferred_element_type=jnp.float32
    )


def product(left, right):
    return jnp.dot(left, right, preferred_element_type=jnp.float32)


def two_heads(left):
    first, second = left[:, :HEAD_DIM], left[:, HEAD_DIM:]
    empty = jnp.zeros_like(first)
    return jnp.concatenate(
        [
            jnp.concatenate([first, empty], axis=1),
            jnp.concatenate([empty, second], axis=1),
        ],
        axis=0,
    )


def pair_rows(left, right):
    both = product_rows(two_heads(left), right)
    return [both[:BLOCK], both[BLOCK:]]


def pair_product(left, right):
    both = product(jnp.concatenate(left, axis=0), right)
    return [both[:BLOCK, :HEAD_DIM], both[BLOCK:, HEAD_DIM:]]


def staged(units, stages, lags):
    for turn in range(len(units) + max(lags)):
        for stage, lag in zip(stages, lags):
            if 0 <= turn - lag < len(units):
                stage(units[turn - lag])


def send_head(copies, head, pairs, sems):
    columns = pl.ds(head * HEAD_DIM, HEAD_DIM)
    for index, (source, target) in enumerate(pairs):
        copy = pltpu.make_async_copy(
            source.at[:, columns],
            target.at[:, columns],
            sems.at[index, head],
        )
        copy.start()
        copies.append(copy)


def query_kernel(hops, first, info, kb, q_ref, k_ref, v_ref, g_ref, *refs):
    behind = refs[: len(hops) + (first > 0)]
    att_ref, dq_ref, stat_ref, bias_ref = refs[-4:]
    heads = att_ref.shape[1] // HEAD_DIM
    base = first
    device, valid = info[0], info[1]
    pieces = 2 + len(hops)

    def rows_ok(block):
        at = (device * 2 + block) * BLOCK
        return at + lax.broadcasted_iota(jnp.int32, (BLOCK, 1), 0) < valid

    if True:
        for block in range(2):
            here = device * 2 + block
            query = lax.broadcasted_iota(jnp.int32, (BLOCK, BLOCK), 0)
            key = lax.broadcasted_iota(jnp.int32, (BLOCK, BLOCK), 1)
            row_ok = here * BLOCK + query < valid
            for piece in range(pieces):
                there = here if piece == 0 else here - 2 ** (piece - 1)
                allowed = row_ok & (there * BLOCK + key < valid)
                if piece == 0:
                    allowed = allowed & (key <= query)
                else:
                    entry = kb[block, piece - 1]
                    allowed = allowed & ((entry >= 0) & (entry == there))
                bias_ref[block, :, piece * BLOCK : (piece + 1) * BLOCK] = jnp.where(
                    allowed, 0.0, -FAR
                )
            level = lax.broadcasted_iota(jnp.int32, (LEVELS, BLOCK), 0)
            row = lax.broadcasted_iota(jnp.int32, (LEVELS, BLOCK), 1)
            flags = jnp.zeros((LEVELS, BLOCK), jnp.float32)
            for index in range(LEVELS):
                entry = kb[block, index]
                hit = ((entry >= 0) & (entry == here - 2**index)).astype(jnp.float32)
                flags = jnp.where(level == index, hit, flags)
            flags = jnp.where(here * BLOCK + row < valid, flags, 0.0)
            stat_ref[3, :, block * BLOCK : (block + 1) * BLOCK] = flags
        if first:
            stat_ref[:3] = behind[-1][:3]

    lane = lax.broadcasted_iota(jnp.int32, (BLOCK, BLOCK), 1)
    units = [(pair, block) for pair in range(heads // 2) for block in range(2)]
    held = {}

    def stack(unit, own_ref, which):
        pair, block = unit

        def part(ref, index):
            shift = first * HEAD_DIM if ref is own_ref else 0
            return ref[
                index * BLOCK : (index + 1) * BLOCK, pl.ds(shift + pair * 2 * HEAD_DIM, 2 * HEAD_DIM)
            ]

        parts = [part(own_ref, block)]
        parts.append(part(behind[0], which * 2 + 1) if block == 0 else part(own_ref, 0))
        parts += [part(ref, which * 2 + block) for ref in behind[: len(hops)]]
        return jnp.concatenate(parts, axis=0)

    def place(unit, shift=0):
        pair, block = unit
        return (
            slice(block * BLOCK, (block + 1) * BLOCK),
            slice((shift + 2 * pair) * HEAD_DIM, (shift + 2 * pair + 2) * HEAD_DIM),
        )

    def products(unit):
        rows, columns = place(unit, first)
        scores = pair_rows(q_ref[rows, columns], stack(unit, k_ref, 0))
        weight_grad = pair_rows(g_ref[rows, columns], stack(unit, v_ref, 1))
        held[unit] = (scores, weight_grad)

    def soften(unit):
        both, weight_grad = held[unit]
        weights, top, inverses = [], [], []
        for scores in both:
            scores = scores * SCALE2 + bias_ref[unit[1]]
            row_max = jnp.max(scores, axis=1, keepdims=True)
            raw = jnp.exp2(scores - row_max)
            total = jnp.sum(raw, axis=1, keepdims=True)
            inverse = jnp.where(rows_ok(unit[1]), 1.0 / total, 0.0)
            weights.append(raw * inverse)
            top.append(jnp.where(rows_ok(unit[1]), row_max, FAR))
            inverses.append(inverse)
        held[unit] = (weights, weight_grad, top, inverses)

    def attend(unit):
        weights, weight_grad, top, inverse = held[unit]
        rows, columns = place(unit)
        attended = pair_product([w.astype(jnp.bfloat16) for w in weights], stack(unit, v_ref, 1))
        attended = jnp.concatenate(attended, axis=1).astype(jnp.bfloat16)
        att_ref[rows, columns] = attended
        terms = g_ref[place(unit, first)].astype(jnp.float32) * attended.astype(jnp.float32)
        deltas = []
        for index in range(2):
            delta = jnp.sum(
                terms[:, index * HEAD_DIM : (index + 1) * HEAD_DIM], axis=1, keepdims=True
            )
            packed = jnp.where(lane == 0, top[index], jnp.where(lane == 1, inverse[index], delta))
            turned = packed.T
            for kind in range(3):
                at = base + 2 * unit[0] + index
                stat_ref[kind, at : at + 1, rows] = turned[kind : kind + 1]
            deltas.append(delta)
        held[unit] = (weights, weight_grad, deltas)

    def finish(unit):
        score_grad = [
            (w * (wg - d)).astype(jnp.bfloat16) for w, wg, d in zip(*held[unit])
        ]
        query_grad = pair_product(score_grad, stack(unit, k_ref, 0))
        dq_ref[place(unit)] = (jnp.concatenate(query_grad, axis=1) * SCALE).astype(jnp.bfloat16)

    staged(units, (products, soften, attend, finish), QUERY_LAG)


def key_stack(hops, chunks, heads, refs):
    count = len(hops)

    def stack(unit, own_ref, which):
        pair, block = unit
        chunk = pair * chunks * 2 // heads
        ahead = refs[chunk * count : (chunk + 1) * count]

        def part(ref, index):
            shift = 0 if ref is own_ref else -chunk * heads // chunks * HEAD_DIM
            return ref[
                index * BLOCK : (index + 1) * BLOCK, pl.ds(shift + pair * 2 * HEAD_DIM, 2 * HEAD_DIM)
            ]

        parts = [part(own_ref, block)]
        parts.append(part(own_ref, 1) if block == 0 else part(ahead[0], 4 + which * 2))
        parts += [
            part(ref, which * 2 + block + (4 if index == 0 else 0)) for index, ref in enumerate(ahead)
        ]
        return jnp.concatenate(parts, axis=0)

    return stack


def product_kernel(hops, chunks, q_ref, k_ref, v_ref, g_ref, *refs):
    score_ref, grad_ref = refs[-2:]
    heads = q_ref.shape[1] // HEAD_DIM
    stack = key_stack(hops, chunks, heads, refs)
    for pair in range(heads // 2):
        for block in range(2):
            rows = slice(block * BLOCK, (block + 1) * BLOCK)
            columns = slice(2 * pair * HEAD_DIM, (2 * pair + 2) * HEAD_DIM)
            unit = (pair, block)
            scores = pair_rows(k_ref[rows, columns], stack(unit, q_ref, 0))
            weight_grad = pair_rows(v_ref[rows, columns], stack(unit, g_ref, 1))
            for index in range(2):
                score_ref[2 * pair + index, rows] = scores[index]
                grad_ref[2 * pair + index, rows] = weight_grad[index]


def key_kernel(hops, chunks, info, score_ref, grad_ref, q_ref, g_ref, *refs):
    count = len(hops)
    stats = refs[chunks * count : (chunks + 1) * count + 1]
    fronts = refs[(chunks + 1) * count + 1 : (chunks + 1) * count + 1 + 2 * chunks]
    att_out, dq_out, dk_out, dv_out, dk_ref, dv_ref, sems, front_sems = refs[-8:]
    heads = dk_ref.shape[1] // HEAD_DIM
    device, valid, devices = info[0], info[1], info[2]
    flags = [ref[3] for ref in stats]
    units = [(pair, block) for pair in range(heads // 2) for block in range(2)]
    held = {}
    stack = key_stack(hops, chunks, heads, refs)

    def place(unit, shift=0):
        pair, block = unit
        return (
            slice(block * BLOCK, (block + 1) * BLOCK),
            slice((shift + 2 * pair) * HEAD_DIM, (shift + 2 * pair + 2) * HEAD_DIM),
        )

    def lanes(array, row, index):
        return array[row : row + 1, index * BLOCK : (index + 1) * BLOCK]

    def soften(unit):
        pair, block = unit
        held[unit] = [
            soften_head(2 * pair + index, block)
            for index in range(2)
        ]

    def soften_head(head, block):
        scores = score_ref[head, block * BLOCK : (block + 1) * BLOCK]
        weight_grad = grad_ref[head, block * BLOCK : (block + 1) * BLOCK]
        stat = [
            [ref[kind, head : head + 1, :] for kind in range(3)] for ref in stats
        ]
        sources = [(0, block, None)]
        sources.append((0, 1, 0) if block == 0 else (1, 0, 0))
        sources += [(1 + index, block, index + 1) for index in range(count)]
        row_max, inverse, delta = [], [], []
        for source, at, level in sources:
            top = lanes(stat[source][0], 0, at)
            if level is not None:
                flag = lanes(flags[source], level, at)
                if source > 0:
                    flag = jnp.where(device + hops[source - 1] < devices, flag, 0.0)
                top = jnp.where(flag > 0.5, top, FAR)
            row_max.append(top)
            inverse.append(lanes(stat[source][1], 0, at))
            delta.append(lanes(stat[source][2], 0, at))
        row_max, inverse, delta = (
            jnp.concatenate(parts, axis=1) for parts in (row_max, inverse, delta)
        )
        scores = scores * SCALE2 - row_max
        key_index = lax.broadcasted_iota(jnp.int32, (BLOCK, BLOCK), 0)
        query_index = lax.broadcasted_iota(jnp.int32, (BLOCK, BLOCK), 1)
        causal = jnp.where(key_index <= query_index, scores[:, :BLOCK], -FAR)
        scores = jnp.concatenate([causal, scores[:, BLOCK:]], axis=1)
        weights = jnp.exp2(scores) * inverse
        score_grad = (weights * (weight_grad - delta)).astype(jnp.bfloat16)
        return (weights.astype(jnp.bfloat16), score_grad)

    def finish(unit):
        weights_low, score_grad = zip(*held[unit])
        rows, columns = place(unit)
        value_grad = jnp.concatenate(pair_product(weights_low, stack(unit, g_ref, 1)), axis=1)
        key_grad = jnp.concatenate(pair_product(score_grad, stack(unit, q_ref, 0)), axis=1) * SCALE
        at = (device * 2 + unit[1]) * BLOCK
        key_ok = at + lax.broadcasted_iota(jnp.int32, (BLOCK, 1), 0) < valid
        dk_ref[rows, columns] = jnp.where(key_ok, key_grad, 0.0).astype(jnp.bfloat16)
        dv_ref[rows, columns] = jnp.where(key_ok, value_grad, 0.0).astype(jnp.bfloat16)
        if unit[1] == 1:
            for head in (2 * unit[0], 2 * unit[0] + 1):
                send_head(copies, head, ((dk_ref, dk_out), (dv_ref, dv_out)), sems)

    copies = []
    for chunk in range(chunks):
        width = dk_ref.shape[1] // chunks
        for index, target in enumerate((att_out, dq_out)):
            copy = pltpu.make_async_copy(
                fronts[2 * chunk + index],
                target.at[:, pl.ds(chunk * width, width)],
                front_sems.at[index, chunk],
            )
            copy.start()
            copies.append(copy)
    staged(units, (soften, finish), KEY_LAG)
    for copy in copies:
        copy.wait()


def mix_kernel(first, info, q_ref, k_ref, v_ref, g_ref, one_ref, two_ref, out_ref, key_ref, query_ref):
    device = info[0]
    rows, width = q_ref.shape[0], one_ref.shape[1]
    columns = slice(first * HEAD_DIM, first * HEAD_DIM + width)
    side, core = (device >> 1) & 1, device & 1

    @pl.when(side == 0)
    def _():
        key_ref[...] = two_ref[...]
        query_ref[...] = one_ref[...]

    @pl.when(side == 1)
    def _():
        key_ref[...] = one_ref[...]
        query_ref[...] = two_ref[...]

    @pl.when(core == 0)
    def _():
        out_ref[:rows] = k_ref[:, columns]
        out_ref[rows : 2 * rows] = v_ref[:, columns]
        out_ref[2 * rows :] = query_ref[...]

    @pl.when(core == 1)
    def _():
        out_ref[: 2 * rows] = key_ref[...]
        out_ref[2 * rows : 3 * rows] = q_ref[:, columns]
        out_ref[3 * rows :] = g_ref[:, columns]


def call(kernel, scalars, arrays, out_shapes, scratch=(), flops=0, to_hbm=False):
    vmem = pl.BlockSpec(memory_space=pltpu.VMEM)
    return pl.pallas_call(
        kernel,
        in_specs=[pl.BlockSpec(memory_space=pltpu.SMEM)] * len(scalars) + [vmem] * len(arrays),
        out_specs=[pl.BlockSpec(memory_space=pl.ANY) if to_hbm else vmem] * len(out_shapes),
        out_shape=out_shapes,
        scratch_shapes=list(scratch),
        cost_estimate=pl.CostEstimate(flops=flops, bytes_accessed=6 << 20, transcendentals=0),
        compiler_params=pltpu.CompilerParams(vmem_limit_bytes=16 << 20),
    )(*scalars, *arrays)


def local(queries, keys, values, out_grad, key_blocks, path_length):
    rows_dev, columns = queries.shape
    head_count = columns // HEAD_DIM
    devices = lax.axis_size("ctx")
    device = lax.axis_index("ctx")
    side, core = (device // 2) % 2, device % 2
    hops = [2**level for level in range(LEVELS - 1) if 2**level < devices]
    info = jnp.stack([device, path_length[0], jnp.int32(devices)]).astype(jnp.int32)

    def up(value, steps):
        return lax.ppermute(value, "ctx", [(at, at + steps) for at in range(devices - steps)])

    def down(value, steps):
        return lax.ppermute(value, "ctx", [(at + steps, at) for at in range(devices - steps)])

    def swap(value, bit):
        return lax.ppermute(value, "ctx", [(at, at ^ bit) for at in range(devices)])

    def back_round(value, steps):
        return lax.ppermute(value, "ctx", [((at + steps) % devices, at) for at in range(devices)])

    heads = head_count // CHUNKS
    width = heads * HEAD_DIM
    packs = []
    for chunk in range(CHUNKS):
        cut = slice(chunk * width, (chunk + 1) * width)
        packs.append(
            (
                jnp.concatenate([keys[:, cut], values[:, cut]], axis=0),
                jnp.concatenate([queries[:, cut], out_grad[:, cut]], axis=0),
            )
        )
    first = []
    for key_pack, query_pack in packs:
        first.append(
            (
                up(key_pack, 4),
                down(query_pack, 4),
                swap(jnp.where(side == 0, key_pack, query_pack), 2),
            )
        )
    own = (queries, keys, values, out_grad)
    full = jax.ShapeDtypeStruct((rows_dev, columns), jnp.bfloat16)
    stat_shape = jax.ShapeDtypeStruct((4, max(head_count, LEVELS), rows_dev), jnp.float32)
    pieces = 2 + len(hops)
    part = jax.ShapeDtypeStruct((rows_dev, width), jnp.bfloat16)
    raw_shape = jax.ShapeDtypeStruct((head_count, rows_dev, pieces * BLOCK), jnp.float32)
    flops = heads * 2 * pieces * 4 * 2 * BLOCK**3

    middle = []
    for (key_pack, query_pack), stage in zip(packs, first):
        key_4, query_4, side_1 = lax.optimization_barrier(stage)
        side_2 = swap(jnp.where(side == 0, query_4, key_4), 2)
        keys_by, queries_by = {4: key_4}, {4: query_4}
        steps = 4
        while steps * 2 < devices:
            keys_by[steps * 2] = up(keys_by[steps], steps)
            queries_by[steps * 2] = down(queries_by[steps], steps)
            steps *= 2
        middle.append((side_1, side_2, keys_by, queries_by))

    front, stats, moved = (), [], []
    for chunk in range(CHUNKS):
        (key_pack, query_pack), (side_1, side_2, keys_by, queries_by) = packs[chunk], middle[chunk]
        side_2, keys_by[8], queries_by[8] = lax.optimization_barrier((side_2, keys_by[8], queries_by[8]))
        packed, keys_by[2], queries_by[2] = call(
            functools.partial(mix_kernel, chunk * heads),
            (info,),
            own + (side_1, side_2),
            (
                jax.ShapeDtypeStruct((4 * rows_dev, width), jnp.bfloat16),
                jax.ShapeDtypeStruct((2 * rows_dev, width), jnp.bfloat16),
                jax.ShapeDtypeStruct((2 * rows_dev, width), jnp.bfloat16),
            ),
        )
        neighbour = swap(packed, 1)
        moved.append(
            (
                [neighbour] + [keys_by[hop] for hop in hops[1:]],
                [neighbour] + [queries_by[hop] for hop in hops[1:]],
            )
        )
        att, dq, stat = call(
            functools.partial(query_kernel, hops, chunk * heads),
            (info, key_blocks),
            own + tuple(moved[chunk][0]) + tuple(stats[-1:]),
            (part, part, stat_shape),
            [pltpu.VMEM((2, BLOCK, pieces * BLOCK), jnp.float32)],
            flops,
        )
        front += (att, dq)
        stats.append(stat)
    stats = (stat,) + tuple(back_round(stat, hop) for hop in hops)
    ahead = sum((tuple(pair[1]) for pair in moved), ())
    raw = call(
        functools.partial(product_kernel, hops, CHUNKS), (), own + ahead, (raw_shape, raw_shape), (), 2 * flops
    )
    return call(
        functools.partial(key_kernel, hops, CHUNKS),
        (info,),
        tuple(raw) + (queries, out_grad) + ahead + stats + front,
        (full,) * 4,
        [
            pltpu.VMEM((rows_dev, columns), jnp.bfloat16),
            pltpu.VMEM((rows_dev, columns), jnp.bfloat16),
            pltpu.SemaphoreType.DMA((2, head_count)),
            pltpu.SemaphoreType.DMA((2, CHUNKS)),
        ],
        2 * flops,
        to_hbm=True,
    )


def solution(mesh):
    placed = (P(("grp", "ctx"), None),) * 5 + (P("grp"),)
    return jax.shard_map(
        local,
        mesh=mesh,
        in_specs=placed,
        out_specs=(P(("grp", "ctx"), None),) * 4,
        check_vma=False,
    )
```

```python
import functools
import math

import jax
import jax.numpy as jnp
from jax import lax
from jax.experimental import pallas as pl
from jax.experimental.pallas import tpu as pltpu
from jax.sharding import PartitionSpec as P

HEAD_DIM = 128
BLOCK = 128
LEVELS = 8
CHUNKS = 2
MARK = 8 * 10**9
QUERY_LAG = (0, 1, 2, 3)
KEY_LAG = (0, 1)
FAR = 1e30
SCALE = HEAD_DIM ** (-0.5)
SCALE2 = SCALE * math.log2(math.e)


def product_rows(left, right):
    return lax.dot_general(
        left, right, (((1,), (1,)), ((), ())), preferred_element_type=jnp.float32
    )


def product(left, right):
    return jnp.dot(left, right, preferred_element_type=jnp.float32)


def two_heads(left):
    first, second = left[:, :HEAD_DIM], left[:, HEAD_DIM:]
    empty = jnp.zeros_like(first)
    return jnp.concatenate(
        [
            jnp.concatenate([first, empty], axis=1),
            jnp.concatenate([empty, second], axis=1),
        ],
        axis=0,
    )


def pair_rows(left, right):
    both = product_rows(two_heads(left), right)
    return [both[:BLOCK], both[BLOCK:]]


def pair_product(left, right):
    both = product(jnp.concatenate(left, axis=0), right)
    return [both[:BLOCK, :HEAD_DIM], both[BLOCK:, HEAD_DIM:]]


def staged(units, stages, lags):
    for turn in range(len(units) + max(lags)):
        for stage, lag in zip(stages, lags):
            if 0 <= turn - lag < len(units):
                stage(units[turn - lag])


def send_head(copies, head, pairs, sems):
    columns = pl.ds(head * HEAD_DIM, HEAD_DIM)
    for index, (source, target) in enumerate(pairs):
        copy = pltpu.make_async_copy(
            source.at[:, columns],
            target.at[:, columns],
            sems.at[index, head],
        )
        copy.start()
        copies.append(copy)


def query_kernel(hops, first, info, kb, q_ref, k_ref, v_ref, g_ref, *refs):
    behind = refs[: len(hops) + (first > 0)]
    att_ref, dq_ref, stat_ref, bias_ref = refs[-4:]
    heads = att_ref.shape[1] // HEAD_DIM
    base = first
    device, valid = info[0], info[1]
    pieces = 2 + len(hops)

    def rows_ok(block):
        at = (device * 2 + block) * BLOCK
        return at + lax.broadcasted_iota(jnp.int32, (BLOCK, 1), 0) < valid

    if True:
        for block in range(2):
            here = device * 2 + block
            query = lax.broadcasted_iota(jnp.int32, (BLOCK, BLOCK), 0)
            key = lax.broadcasted_iota(jnp.int32, (BLOCK, BLOCK), 1)
            row_ok = here * BLOCK + query < valid
            for piece in range(pieces):
                there = here if piece == 0 else here - 2 ** (piece - 1)
                allowed = row_ok & (there * BLOCK + key < valid)
                if piece == 0:
                    allowed = allowed & (key <= query)
                else:
                    entry = kb[block, piece - 1]
                    allowed = allowed & ((entry >= 0) & (entry == there))
                bias_ref[block, :, piece * BLOCK : (piece + 1) * BLOCK] = jnp.where(
                    allowed, 0.0, -FAR
                )
            level = lax.broadcasted_iota(jnp.int32, (LEVELS, BLOCK), 0)
            row = lax.broadcasted_iota(jnp.int32, (LEVELS, BLOCK), 1)
            flags = jnp.zeros((LEVELS, BLOCK), jnp.float32)
            for index in range(LEVELS):
                entry = kb[block, index]
                hit = ((entry >= 0) & (entry == here - 2**index)).astype(jnp.float32)
                flags = jnp.where(level == index, hit, flags)
            flags = jnp.where(here * BLOCK + row < valid, flags, 0.0)
            stat_ref[3, :, block * BLOCK : (block + 1) * BLOCK] = flags
        if first:
            stat_ref[:3] = behind[-1][:3]

    lane = lax.broadcasted_iota(jnp.int32, (BLOCK, BLOCK), 1)
    units = [(pair, block) for pair in range(heads // 2) for block in range(2)]
    held = {}

    def stack(unit, own_ref, which):
        pair, block = unit

        def part(ref, index):
            shift = first * HEAD_DIM if ref is own_ref else 0
            return ref[
                index * BLOCK : (index + 1) * BLOCK, pl.ds(shift + pair * 2 * HEAD_DIM, 2 * HEAD_DIM)
            ]

        parts = [part(own_ref, block)]
        parts.append(part(behind[0], which * 2 + 1) if block == 0 else part(own_ref, 0))
        parts += [part(ref, which * 2 + block) for ref in behind[: len(hops)]]
        return jnp.concatenate(parts, axis=0)

    def place(unit, shift=0):
        pair, block = unit
        return (
            slice(block * BLOCK, (block + 1) * BLOCK),
            slice((shift + 2 * pair) * HEAD_DIM, (shift + 2 * pair + 2) * HEAD_DIM),
        )

    def products(unit):
        rows, columns = place(unit, first)
        scores = pair_rows(q_ref[rows, columns], stack(unit, k_ref, 0))
        weight_grad = pair_rows(g_ref[rows, columns], stack(unit, v_ref, 1))
        held[unit] = (scores, weight_grad)

    def soften(unit):
        both, weight_grad = held[unit]
        weights, top, inverses = [], [], []
        for scores in both:
            scores = scores * SCALE2 + bias_ref[unit[1]]
            row_max = jnp.max(scores, axis=1, keepdims=True)
            raw = jnp.exp2(scores - row_max)
            total = jnp.sum(raw, axis=1, keepdims=True)
            inverse = jnp.where(rows_ok(unit[1]), 1.0 / total, 0.0)
            weights.append(raw * inverse)
            top.append(jnp.where(rows_ok(unit[1]), row_max, FAR))
            inverses.append(inverse)
        held[unit] = (weights, weight_grad, top, inverses)

    def attend(unit):
        weights, weight_grad, top, inverse = held[unit]
        rows, columns = place(unit)
        attended = pair_product([w.astype(jnp.bfloat16) for w in weights], stack(unit, v_ref, 1))
        attended = jnp.concatenate(attended, axis=1).astype(jnp.bfloat16)
        att_ref[rows, columns] = attended
        terms = g_ref[place(unit, first)].astype(jnp.float32) * attended.astype(jnp.float32)
        deltas = []
        for index in range(2):
            delta = jnp.sum(
                terms[:, index * HEAD_DIM : (index + 1) * HEAD_DIM], axis=1, keepdims=True
            )
            packed = jnp.where(lane == 0, top[index], jnp.where(lane == 1, inverse[index], delta))
            turned = packed.T
            for kind in range(3):
                at = base + 2 * unit[0] + index
                stat_ref[kind, at : at + 1, rows] = turned[kind : kind + 1]
            deltas.append(delta)
        held[unit] = (weights, weight_grad, deltas)

    def finish(unit):
        score_grad = [
            (w * (wg - d)).astype(jnp.bfloat16) for w, wg, d in zip(*held[unit])
        ]
        query_grad = pair_product(score_grad, stack(unit, k_ref, 0))
        dq_ref[place(unit)] = (jnp.concatenate(query_grad, axis=1) * SCALE).astype(jnp.bfloat16)

    staged(units, (products, soften, attend, finish), QUERY_LAG)


def key_stack(hops, chunks, heads, refs):
    count = len(hops)

    def stack(unit, own_ref, which):
        pair, block = unit
        chunk = pair * chunks * 2 // heads
        ahead = refs[chunk * count : (chunk + 1) * count]

        def part(ref, index):
            shift = 0 if ref is own_ref else -chunk * heads // chunks * HEAD_DIM
            return ref[
                index * BLOCK : (index + 1) * BLOCK, pl.ds(shift + pair * 2 * HEAD_DIM, 2 * HEAD_DIM)
            ]

        parts = [part(own_ref, block)]
        parts.append(part(own_ref, 1) if block == 0 else part(ahead[0], 4 + which * 2))
        parts += [
            part(ref, which * 2 + block + (4 if index == 0 else 0)) for index, ref in enumerate(ahead)
        ]
        return jnp.concatenate(parts, axis=0)

    return stack


def product_kernel(hops, chunks, q_ref, k_ref, v_ref, g_ref, *refs):
    score_ref, grad_ref = refs[-2:]
    heads = q_ref.shape[1] // HEAD_DIM
    stack = key_stack(hops, chunks, heads, refs)
    for pair in range(heads // 2):
        for block in range(2):
            rows = slice(block * BLOCK, (block + 1) * BLOCK)
            columns = slice(2 * pair * HEAD_DIM, (2 * pair + 2) * HEAD_DIM)
            unit = (pair, block)
            scores = pair_rows(k_ref[rows, columns], stack(unit, q_ref, 0))
            weight_grad = pair_rows(v_ref[rows, columns], stack(unit, g_ref, 1))
            for index in range(2):
                score_ref[2 * pair + index, rows] = scores[index]
                grad_ref[2 * pair + index, rows] = weight_grad[index]


def key_kernel(hops, chunks, info, score_ref, grad_ref, q_ref, g_ref, *refs):
    count = len(hops)
    stats = refs[chunks * count : (chunks + 1) * count + 1]
    fronts = refs[(chunks + 1) * count + 1 : (chunks + 1) * count + 1 + 2 * chunks]
    att_out, dq_out, dk_out, dv_out, dk_ref, dv_ref, sems, front_sems = refs[-8:]
    heads = dk_ref.shape[1] // HEAD_DIM
    device, valid, devices = info[0], info[1], info[2]
    flags = [ref[3] for ref in stats]
    units = [(pair, block) for pair in range(heads // 2) for block in range(2)]
    held = {}
    stack = key_stack(hops, chunks, heads, refs)

    def place(unit, shift=0):
        pair, block = unit
        return (
            slice(block * BLOCK, (block + 1) * BLOCK),
            slice((shift + 2 * pair) * HEAD_DIM, (shift + 2 * pair + 2) * HEAD_DIM),
        )

    def lanes(array, row, index):
        return array[row : row + 1, index * BLOCK : (index + 1) * BLOCK]

    def soften(unit):
        pair, block = unit
        held[unit] = [
            soften_head(2 * pair + index, block)
            for index in range(2)
        ]

    def soften_head(head, block):
        scores = score_ref[head, block * BLOCK : (block + 1) * BLOCK]
        weight_grad = grad_ref[head, block * BLOCK : (block + 1) * BLOCK]
        stat = [
            [ref[kind, head : head + 1, :] for kind in range(3)] for ref in stats
        ]
        sources = [(0, block, None)]
        sources.append((0, 1, 0) if block == 0 else (1, 0, 0))
        sources += [(1 + index, block, index + 1) for index in range(count)]
        row_max, inverse, delta = [], [], []
        for source, at, level in sources:
            top = lanes(stat[source][0], 0, at)
            if level is not None:
                flag = lanes(flags[source], level, at)
                if source > 0:
                    flag = jnp.where(device + hops[source - 1] < devices, flag, 0.0)
                top = jnp.where(flag > 0.5, top, FAR)
            row_max.append(top)
            inverse.append(lanes(stat[source][1], 0, at))
            delta.append(lanes(stat[source][2], 0, at))
        row_max, inverse, delta = (
            jnp.concatenate(parts, axis=1) for parts in (row_max, inverse, delta)
        )
        scores = scores * SCALE2 - row_max
        key_index = lax.broadcasted_iota(jnp.int32, (BLOCK, BLOCK), 0)
        query_index = lax.broadcasted_iota(jnp.int32, (BLOCK, BLOCK), 1)
        causal = jnp.where(key_index <= query_index, scores[:, :BLOCK], -FAR)
        scores = jnp.concatenate([causal, scores[:, BLOCK:]], axis=1)
        weights = jnp.exp2(scores) * inverse
        score_grad = (weights * (weight_grad - delta)).astype(jnp.bfloat16)
        return (weights.astype(jnp.bfloat16), score_grad)

    def finish(unit):
        weights_low, score_grad = zip(*held[unit])
        rows, columns = place(unit)
        value_grad = jnp.concatenate(pair_product(weights_low, stack(unit, g_ref, 1)), axis=1)
        key_grad = jnp.concatenate(pair_product(score_grad, stack(unit, q_ref, 0)), axis=1) * SCALE
        at = (device * 2 + unit[1]) * BLOCK
        key_ok = at + lax.broadcasted_iota(jnp.int32, (BLOCK, 1), 0) < valid
        dk_ref[rows, columns] = jnp.where(key_ok, key_grad, 0.0).astype(jnp.bfloat16)
        dv_ref[rows, columns] = jnp.where(key_ok, value_grad, 0.0).astype(jnp.bfloat16)
        if unit[1] == 1:
            for head in (2 * unit[0], 2 * unit[0] + 1):
                send_head(copies, head, ((dk_ref, dk_out), (dv_ref, dv_out)), sems)

    copies = []
    for chunk in range(chunks):
        width = dk_ref.shape[1] // chunks
        for index, target in enumerate((att_out, dq_out)):
            copy = pltpu.make_async_copy(
                fronts[2 * chunk + index],
                target.at[:, pl.ds(chunk * width, width)],
                front_sems.at[index, chunk],
            )
            copy.start()
            copies.append(copy)
    staged(units, (soften, finish), KEY_LAG)
    for copy in copies:
        copy.wait()


def mark_kernel(in_ref, out_ref):
    out_ref[...] = in_ref[...]


def mix_kernel(first, info, kb, q_ref, k_ref, v_ref, g_ref, one_ref, two_ref, out_ref, key_ref, query_ref):
    device = info[0]
    rows, width = q_ref.shape[0], one_ref.shape[1]
    columns = slice(first * HEAD_DIM, first * HEAD_DIM + width)
    side, core = (device >> 1) & 1, device & 1

    @pl.when(side == 0)
    def _():
        key_ref[...] = two_ref[...]
        query_ref[...] = one_ref[...]

    @pl.when(side == 1)
    def _():
        key_ref[...] = one_ref[...]
        query_ref[...] = two_ref[...]

    @pl.when(core == 0)
    def _():
        out_ref[:rows] = k_ref[:, columns]
        out_ref[rows : 2 * rows] = v_ref[:, columns]
        out_ref[2 * rows :] = query_ref[...]

    @pl.when(core == 1)
    def _():
        out_ref[: 2 * rows] = key_ref[...]
        out_ref[2 * rows : 3 * rows] = q_ref[:, columns]
        out_ref[3 * rows :] = g_ref[:, columns]


def call(kernel, scalars, arrays, out_shapes, scratch=(), flops=0, to_hbm=False):
    vmem = pl.BlockSpec(memory_space=pltpu.VMEM)
    return pl.pallas_call(
        kernel,
        in_specs=[pl.BlockSpec(memory_space=pltpu.SMEM)] * len(scalars) + [vmem] * len(arrays),
        out_specs=[pl.BlockSpec(memory_space=pl.ANY) if to_hbm else vmem] * len(out_shapes),
        out_shape=out_shapes,
        scratch_shapes=list(scratch),
        cost_estimate=pl.CostEstimate(flops=flops, bytes_accessed=0, transcendentals=0),
        compiler_params=pltpu.CompilerParams(vmem_limit_bytes=16 << 20),
    )(*scalars, *arrays)


def local(queries, keys, values, out_grad, key_blocks, path_length):
    rows_dev, columns = queries.shape
    head_count = columns // HEAD_DIM
    devices = lax.axis_size("ctx")
    device = lax.axis_index("ctx")
    side, core = (device // 2) % 2, device % 2
    hops = [2**level for level in range(LEVELS - 1) if 2**level < devices]
    info = jnp.stack([device, path_length[0], jnp.int32(devices)]).astype(jnp.int32)

    def up(value, steps):
        return lax.ppermute(value, "ctx", [(at, at + steps) for at in range(devices - steps)])

    def down(value, steps):
        return lax.ppermute(value, "ctx", [(at + steps, at) for at in range(devices - steps)])

    def swap(value, bit):
        return lax.ppermute(value, "ctx", [(at, at ^ bit) for at in range(devices)])

    def back_round(value, steps):
        return lax.ppermute(value, "ctx", [((at + steps) % devices, at) for at in range(devices)])

    heads = head_count // CHUNKS
    width = heads * HEAD_DIM
    packs = []
    for chunk in range(CHUNKS):
        cut = slice(chunk * width, (chunk + 1) * width)
        packs.append(
            (
                jnp.concatenate([keys[:, cut], values[:, cut]], axis=0),
                jnp.concatenate([queries[:, cut], out_grad[:, cut]], axis=0),
            )
        )
    first = []
    for key_pack, query_pack in packs:
        first.append(
            (
                up(key_pack, 4),
                down(query_pack, 4),
                swap(jnp.where(side == 0, key_pack, query_pack), 2),
            )
        )
    own = (queries, keys, values, out_grad)
    full = jax.ShapeDtypeStruct((rows_dev, columns), jnp.bfloat16)
    stat_shape = jax.ShapeDtypeStruct((4, max(head_count, LEVELS), rows_dev), jnp.float32)
    pieces = 2 + len(hops)
    part = jax.ShapeDtypeStruct((rows_dev, width), jnp.bfloat16)
    raw_shape = jax.ShapeDtypeStruct((head_count, rows_dev, pieces * BLOCK), jnp.float32)
    flops = heads * 2 * pieces * 4 * 2 * BLOCK**3

    middle = []
    for (key_pack, query_pack), stage in zip(packs, first):
        key_4, query_4, side_1 = lax.optimization_barrier(stage)
        side_2 = swap(jnp.where(side == 0, query_4, key_4), 2)
        keys_by, queries_by = {4: key_4}, {4: query_4}
        steps = 4
        while steps * 2 < devices:
            keys_by[steps * 2] = up(keys_by[steps], steps)
            queries_by[steps * 2] = down(queries_by[steps], steps)
            steps *= 2
        middle.append((side_1, side_2, keys_by, queries_by))

    front, stats, moved = (), [], []
    for chunk in range(CHUNKS):
        (key_pack, query_pack), (side_1, side_2, keys_by, queries_by) = packs[chunk], middle[chunk]
        if chunk < CHUNKS - 1:
            side_2, keys_by[8], queries_by[8] = lax.optimization_barrier(
                (side_2, keys_by[8], queries_by[8])
            )
        packed, keys_by[2], queries_by[2] = call(
            functools.partial(mix_kernel, chunk * heads),
            (info, key_blocks),
            own + (side_1, side_2),
            (
                jax.ShapeDtypeStruct((4 * rows_dev, width), jnp.bfloat16),
                jax.ShapeDtypeStruct((2 * rows_dev, width), jnp.bfloat16),
                jax.ShapeDtypeStruct((2 * rows_dev, width), jnp.bfloat16),
            ),
        )
        neighbour = swap(packed, 1)
        moved.append(
            (
                [neighbour] + [keys_by[hop] for hop in hops[1:]],
                [neighbour] + [queries_by[hop] for hop in hops[1:]],
            )
        )
    mark = jnp.zeros((8, 128), jnp.float32)
    at = hops.index(8)
    moved[-1][0][at], moved[-1][1][at], mark = lax.optimization_barrier(
        (moved[-1][0][at], moved[-1][1][at], mark)
    )
    mark = call(mark_kernel, (), (mark,), [jax.ShapeDtypeStruct(mark.shape, mark.dtype)], (), MARK)[0]
    for chunk in range(CHUNKS):
        att, dq, stat = call(
            functools.partial(query_kernel, hops, chunk * heads),
            (info, key_blocks),
            own + tuple(moved[chunk][0]) + (tuple(stats[-1:]) or (mark,)),
            (part, part, stat_shape),
            [pltpu.VMEM((2, BLOCK, pieces * BLOCK), jnp.float32)],
            flops,
        )
        front += (att, dq)
        stats.append(stat)
    stats = (stat,) + tuple(back_round(stat, hop) for hop in hops)
    ahead = sum((tuple(pair[1]) for pair in moved), ())
    raw = call(
        functools.partial(product_kernel, hops, CHUNKS), (), own + ahead, (raw_shape, raw_shape), (), 2 * flops
    )
    return call(
        functools.partial(key_kernel, hops, CHUNKS),
        (info,),
        tuple(raw) + (queries, out_grad) + ahead + stats + front,
        (full,) * 4,
        [
            pltpu.VMEM((rows_dev, columns), jnp.bfloat16),
            pltpu.VMEM((rows_dev, columns), jnp.bfloat16),
            pltpu.SemaphoreType.DMA((2, head_count)),
            pltpu.SemaphoreType.DMA((2, CHUNKS)),
        ],
        2 * flops,
        to_hbm=True,
    )


def solution(mesh):
    placed = (P(("grp", "ctx"), None),) * 5 + (P("grp"),)
    return jax.shard_map(
        local,
        mesh=mesh,
        in_specs=placed,
        out_specs=(P(("grp", "ctx"), None),) * 4,
        check_vma=False,
    )
```
